32 devices in a mesh: seq: 8 (over y, x, core), head: 4 (over z).
Axes of the slice: x: 2, y: 2, z: 4, core: 2. Of those that a mesh axis runs over, the one named last changes fastest.
Arguments:
- queries: bfloat16 [6144, 2048], P(('seq', 'head')), may hold values from -8 to 8
- keys: bfloat16 [6144, 2048], P(('seq', 'head')), may hold values from -8 to 8
- values: bfloat16 [6144, 2048], P(('seq', 'head')), may hold values from -6 to 6
- cotangent: bfloat16 [6144, 2048], P(('seq', 'head')), may hold values from -6 to 6
- neighbours: int32 [96, 27], replicated, may hold values from -1 to 95, as said below
Outputs:
- output: bfloat16 [6144, 2048], P(('seq', 'head'))
- grad_query: bfloat16 [6144, 2048], P(('seq', 'head'))
- grad_key: bfloat16 [6144, 2048], P(('seq', 'head'))
- grad_value: bfloat16 [6144, 2048], P(('seq', 'head'))
The draws below stay inside these ranges and needn't reach their ends.
Inputs may be any that keep to these rules, and one draw needn't show every extreme that they name: `neighbours`: row g lists distinct tiles, always g itself; a listed tile's frame, tile row and tile column each differ from g's by at most one; -1 marks an empty slot; slots stand in any order.
All inputs are finite; a program needn't handle non-finite values.
Results may differ from the reference program's by a relative error of at most 0.015.
Values may be sent and summed in bfloat16 or wider, within the bound.
A program may use at most 128 MiB of HBM per device.

```python
import math
import jax
import jax.numpy as jnp
from jax import lax

TILE = 64
TILE_ROWS = 3
TILE_COLS = 4
TILES_F = 12
SLOTS = 27
HEADS = 16
HD = 128
FRAMES = 8
TILES = 96
TOKENS = 6144


def shared_pair(key):
    key_query, key_keys = jax.random.split(key, 2)
    width_all = HEADS * HD
    query_draw = 1.5 * jnp.clip(jax.random.normal(key_query, (TOKENS, width_all), jnp.float32), -3.3, 3.3)
    keys_draw = 1.5 * jnp.clip(jax.random.normal(key_keys, (TOKENS, width_all), jnp.float32), -3.3, 3.3)
    return (query_draw, keys_draw)


def draw_queries(key, part):
    query_draw, keys_draw = shared_pair(jax.random.fold_in(key, 7))
    return query_draw.astype(jnp.bfloat16)


def draw_keys(key, part):
    query_draw, keys_draw = shared_pair(jax.random.fold_in(key, 7))
    return keys_draw.astype(jnp.bfloat16)


def draw_neighbours(key, part):
    key_drop, key_order = jax.random.split(jax.random.fold_in(key, 13))
    tile_ids = jnp.arange(TILES, dtype=jnp.int32)
    frame = tile_ids // TILES_F
    tile_row = tile_ids % TILES_F // TILE_COLS
    tile_col = tile_ids % TILE_COLS
    slot = jnp.arange(SLOTS, dtype=jnp.int32)
    step_frame = slot // 9 - 1
    step_row = slot // 3 % 3 - 1
    step_col = slot % 3 - 1
    near_frame = frame[:, None] + step_frame[None, :]
    near_row = tile_row[:, None] + step_row[None, :]
    near_col = tile_col[:, None] + step_col[None, :]
    inside = (near_frame >= 0) & (near_frame < FRAMES) & (near_row >= 0) & (near_row < TILE_ROWS) & (near_col >= 0) & (near_col < TILE_COLS)
    kept = (jax.random.randint(key_drop, (TILES, SLOTS), 0, 4) > 0) | (slot[None, :] == 13)
    listed = jnp.where(inside & kept, near_frame * TILES_F + near_row * TILE_COLS + near_col, -1)
    order_keys = jax.random.randint(key_order, (TILES, SLOTS), 0, 1 << 20) * 32 + slot[None, :]
    order = jnp.argsort(order_keys, axis=1)
    return jnp.take_along_axis(listed, order, axis=1).astype(jnp.int32)


def shard_levels(key, extent, cuts, low, top_value):
    factor_of, own = 1.0, jax.random.fold_in(key, 6)
    for dim, parts in cuts:
        steps = jnp.exp(jax.random.uniform(jax.random.fold_in(own, dim), (parts,), jnp.float32, low / len(cuts), top_value / len(cuts)))
        factor_of = factor_of * jnp.repeat(steps, extent[dim] // parts).reshape([-1 if axis == dim else 1 for axis in range(len(extent))])
    return factor_of


def normal_values(stream_key, dims, width, bound, cuts=(), kind=jnp.bfloat16):
    entries = jax.random.normal(stream_key, dims, jnp.float32) * width
    if len(cuts) > 0:
        entries = shard_levels(stream_key, dims, cuts, -0.22, 0.18) * entries
    return jnp.clip(entries, min=-bound, max=bound).astype(kind)


def setup_inputs(seed: int = 0) -> dict:
    key_list = jax.random.split(jax.random.key(seed), 6)
    return {
        "queries": draw_queries(jax.random.fold_in(key_list[5], 71), 0),
        "keys": draw_keys(jax.random.fold_in(key_list[5], 71), 0),
        "values": normal_values(key_list[2], (TOKENS, HEADS * HD), 1.0, 6.0, ((0, 32),)),
        "cotangent": normal_values(key_list[3], (TOKENS, HEADS * HD), 1.0, 6.0, ((0, 32),)),
        "neighbours": draw_neighbours(jax.random.fold_in(key_list[5], 71), 0),
    }


masked_score = -1e+30

def attend_tiles(query_blk, kv_near, key_mask, cot_blk, head_count):
    block_tiles, tile_len, feature_width = query_blk.shape
    key_len = kv_near.shape[1]
    head_size = feature_width // head_count
    score_scale = 1.0 / math.sqrt(head_size)
    highest = lax.Precision.HIGHEST
    query_heads = query_blk.astype(jnp.float32).reshape(block_tiles, tile_len, head_count, head_size)
    key_heads = kv_near[:, :, :feature_width].astype(jnp.float32).reshape(block_tiles, key_len, head_count, head_size)
    value_heads = kv_near[:, :, feature_width:].astype(jnp.float32).reshape(block_tiles, key_len, head_count, head_size)
    cot_heads = cot_blk.astype(jnp.float32).reshape(block_tiles, tile_len, head_count, head_size)
    scores = jnp.einsum('btnd,bknd->bntk', query_heads, key_heads, precision=highest) * score_scale
    scores = jnp.where(key_mask[:, None, None, :], scores, masked_score)
    row_max = lax.optimization_barrier(jnp.max(scores, axis=-1, keepdims=True))
    log_total = row_max + jnp.log(lax.optimization_barrier(jnp.sum(jnp.exp(scores - row_max), axis=-1, keepdims=True)))
    probs = jnp.exp(scores - log_total)
    probs_low = probs.astype(jnp.bfloat16)
    output = jnp.einsum('bntk,bknd->btnd', probs_low.astype(jnp.float32), value_heads, precision=highest).astype(jnp.bfloat16)
    grad_dot = lax.optimization_barrier(jnp.sum(cot_heads * output.astype(jnp.float32), axis=-1))
    grad_prob = jnp.einsum('btnd,bknd->bntk', cot_heads, value_heads, precision=highest)
    grad_score = (probs * (grad_prob - jnp.transpose(grad_dot, (0, 2, 1))[..., None]) * score_scale).astype(jnp.bfloat16)
    grad_query = jnp.einsum('bntk,bknd->btnd', grad_score.astype(jnp.float32), key_heads, precision=highest).astype(jnp.bfloat16)
    grad_key = jnp.einsum('bntk,btnd->bknd', grad_score.astype(jnp.float32), query_heads, precision=highest)
    grad_value = jnp.einsum('bntk,btnd->bknd', probs_low.astype(jnp.float32), cot_heads, precision=highest)
    grad_pair = jnp.concatenate([grad_key.reshape(block_tiles, key_len, feature_width), grad_value.reshape(block_tiles, key_len, feature_width)], axis=-1)
    return (output.reshape(block_tiles, tile_len, feature_width), grad_query.reshape(block_tiles, tile_len, feature_width), grad_pair)

def reference(queries, keys, values, cotangent, neighbours):
    feature_width = queries.shape[1]
    query_tiles = queries.reshape(TILES, TILE, feature_width)
    cot_tiles = cotangent.reshape(TILES, TILE, feature_width)
    pair_tiles = jnp.concatenate([keys, values], axis=1).reshape(TILES, TILE, 2 * feature_width)
    pair_tiles = jnp.concatenate([pair_tiles, jnp.zeros((1, TILE, 2 * feature_width), pair_tiles.dtype)], axis=0)
    listed = neighbours >= 0
    slot_index = jnp.where(listed, neighbours, TILES).astype(jnp.int32)
    block_tiles = TILES_F // 4

    def one_block(grad_buffer, block_id):
        first_tile = (block_id * block_tiles).astype(jnp.int32)
        query_blk = lax.dynamic_slice_in_dim(query_tiles, first_tile, block_tiles, 0)
        cot_blk = lax.dynamic_slice_in_dim(cot_tiles, first_tile, block_tiles, 0)
        index_blk = lax.dynamic_slice_in_dim(slot_index, first_tile, block_tiles, 0)
        listed_blk = lax.dynamic_slice_in_dim(listed, first_tile, block_tiles, 0)
        kv_near = jnp.take(pair_tiles, index_blk, axis=0).reshape(block_tiles, SLOTS * TILE, 2 * feature_width)
        key_mask = jnp.repeat(listed_blk, TILE, axis=1)
        output, grad_query, grad_pair = attend_tiles(query_blk, kv_near, key_mask, cot_blk, HEADS)
        grad_buffer = grad_buffer.at[index_blk].add(grad_pair.reshape(block_tiles, SLOTS, TILE, 2 * feature_width))
        return (grad_buffer, (output, grad_query))
    start_buffer = jnp.zeros((TILES + 1, TILE, 2 * feature_width), jnp.float32)
    grad_buffer, (outputs, grad_queries) = lax.scan(one_block, start_buffer, jnp.arange(TILES // block_tiles, dtype=jnp.int32))
    output = outputs.reshape(TOKENS, feature_width)
    grad_query = grad_queries.reshape(TOKENS, feature_width)
    grad_rows = grad_buffer[:TILES].reshape(TOKENS, 2 * feature_width)
    return (output, grad_query, grad_rows[:, :feature_width].astype(jnp.bfloat16), grad_rows[:, feature_width:].astype(jnp.bfloat16))
```

```python
import functools
import math

import jax
import jax.numpy as jnp
from jax import lax
from jax.experimental import pallas as pl
from jax.experimental.pallas import tpu as pltpu
from jax.sharding import PartitionSpec as P

TILE = 64
TILE_ROWS = 3
TILE_COLS = 4
TILES_F = 12
HD = 128
FRAME = TILE * TILES_F
ROW = TILE * TILE_COLS
MESH = pl.DeviceIdType.MESH
masked_score = -1e30
F32 = jnp.float32
BF16 = jnp.bfloat16

NT = (((1,), (1,)), ((), ()))
TN = (((0,), (0,)), ((), ()))
NN = (((1,), (0,)), ((), ()))


def dot(a, b, dims):
    return lax.dot_general(a, b, dims, preferred_element_type=F32)


def kernel(
    nseq, nz, heads, rows,
    k_in, v_in, q_in, c_in, bias_ref,
    o_out, gq_out, gk_out, gv_out,
    kx, vx, qb, cb, o_st, gq_st, gk_st, gv_st, g_out, g_in, s_buf, gk_acc, gv_acc,
    in_send, in_recv, in_loc, halo_send, halo_recv, g_send, g_recv, out_send, out_recv, out_loc,
):
    s = lax.axis_index("seq")
    z = lax.axis_index("head")
    has_prev = s > 0
    has_next = s < nseq - 1
    scale = 1.0 / math.sqrt(HD)
    log2_scale = scale * math.log2(math.e)

    peers = [lax.rem(z + d, nz) for d in range(1, nz)]
    ins = (k_in, v_in, q_in, c_in)
    outs = (o_out, gq_out, gk_out, gv_out)
    stages = (o_st, gq_st, gk_st, gv_st)

    def in_place(a, h, source):
        if a < 2:
            start = FRAME + source * rows
            return (kx, vx)[a].at[h, pl.ds(pl.multiple_of(start, 32), rows), :]
        return (qb, cb)[a - 2].at[h, pl.ds(pl.multiple_of(source * rows, 32), rows), :]

    def columns(owner, h):
        return pl.ds(pl.multiple_of((owner * heads + h) * HD, HD), HD)

    def in_copy(a, h, peer, source):
        return pltpu.make_async_remote_copy(
            src_ref=ins[a].at[:, columns(peer, h)],
            dst_ref=in_place(a, h, source),
            send_sem=in_send.at[a, h, peer],
            recv_sem=in_recv.at[a, h, source],
            device_id=(s, peer),
            device_id_type=MESH,
        )

    def in_local(a, h):
        return pltpu.make_async_copy(
            ins[a].at[:, columns(z, h)], in_place(a, h, z), in_loc.at[a, h]
        )

    def out_copy(a, h, peer, source):
        return pltpu.make_async_remote_copy(
            src_ref=stages[a].at[h, pl.ds(pl.multiple_of(peer * rows, 32), rows), :],
            dst_ref=outs[a].at[:, columns(source, h)],
            send_sem=out_send.at[a, h, peer],
            recv_sem=out_recv.at[a, h, source],
            device_id=(s, peer),
            device_id_type=MESH,
        )

    def out_local(a, h):
        return pltpu.make_async_copy(
            stages[a].at[h, pl.ds(pl.multiple_of(z * rows, 32), rows), :],
            outs[a].at[:, columns(z, h)],
            out_loc.at[a, h],
        )

    def halo_copy(a, h, side):
        ext = (kx, vx)[a]
        return pltpu.make_async_remote_copy(
            src_ref=ext.at[h, pl.ds(FRAME, FRAME), :],
            dst_ref=ext.at[h, pl.ds(2 * FRAME * side, FRAME), :],
            send_sem=halo_send.at[a, h, side],
            recv_sem=halo_recv.at[a, h, side],
            device_id=(s + 1 - 2 * side, z),
            device_id_type=MESH,
        )

    def grad_copy(a, h, side):
        return pltpu.make_async_remote_copy(
            src_ref=g_out.at[a, h, side],
            dst_ref=g_in.at[a, h, side],
            send_sem=g_send.at[a, h, side],
            recv_sem=g_recv.at[a, h, side],
            device_id=(s - 1 + 2 * side, z),
            device_id_type=MESH,
        )

    barrier = pltpu.get_barrier_semaphore()
    for peer in peers:
        pl.semaphore_signal(barrier, inc=1, device_id=(s, peer), device_id_type=MESH)

    @pl.when(has_prev)
    def _():
        pl.semaphore_signal(barrier, inc=1, device_id=(s - 1, z), device_id_type=MESH)

    @pl.when(has_next)
    def _():
        pl.semaphore_signal(barrier, inc=1, device_id=(s + 1, z), device_id_type=MESH)

    pl.semaphore_wait(barrier, nz - 1 + has_prev.astype(jnp.int32) + has_next.astype(jnp.int32))

    def start_in(h, _):
        for a in range(4):
            for peer in peers:
                in_copy(a, h, peer, z).start()
            in_local(a, h).start()
        return 0

    lax.fori_loop(0, heads, start_in, 0)

    @pl.when(jnp.logical_not(has_prev))
    def _():
        kx[:, 0:FRAME, :] = jnp.zeros((heads, FRAME, HD), BF16)
        vx[:, 0:FRAME, :] = jnp.zeros((heads, FRAME, HD), BF16)

    @pl.when(jnp.logical_not(has_next))
    def _():
        kx[:, 2 * FRAME : 3 * FRAME, :] = jnp.zeros((heads, FRAME, HD), BF16)
        vx[:, 2 * FRAME : 3 * FRAME, :] = jnp.zeros((heads, FRAME, HD), BF16)

    def wait_in(h, arrays):
        for a in arrays:
            for peer in peers:
                in_copy(a, h, peer, peer).wait_recv()
            in_local(a, h).wait()

    def forward(h):
        wait_in(h, (0, 1))
        for side, there in ((0, has_next), (1, has_prev)):
            @pl.when(there)
            def _(side=side):
                for a in range(2):
                    halo_copy(a, h, side).start()

    def attend(h, r):
        low, high = max(r - 1, 0), min(r + 1, TILE_ROWS - 1)
        near = range(low, high + 1)
        base = r * ROW
        q = qb[h, base : base + ROW, :]
        c = cb[h, base : base + ROW, :]

        def first(f, top):
            for n in near:
                start = pl.multiple_of(f * FRAME + n * ROW, ROW)
                t = dot(kx[h, pl.ds(start, ROW), :], q, NT) * log2_scale
                rows_bias = bias_ref[r, f * TILE_ROWS + n]
                parts = []
                for k in range(TILE_COLS):
                    part = t[k * TILE : (k + 1) * TILE, :] + rows_bias[k : k + 1, :]
                    s_buf[pl.ds(start + k * TILE, TILE), :] = part
                    top = jnp.maximum(top, jnp.max(part.reshape(TILE // 8, 8, ROW), axis=0))
            return top

        top = lax.fori_loop(0, 3, first, jnp.full((8, ROW), masked_score, F32))
        top = jnp.max(top, axis=0, keepdims=True)

        def second(f, carry):
            total, out_t = carry
            for n in near:
                start = pl.multiple_of(f * FRAME + n * ROW, ROW)
                e = jnp.exp2(s_buf[pl.ds(start, ROW), :] - top)
                s_buf[pl.ds(start, ROW), :] = e
                total = total + jnp.sum(e.reshape(ROW // 8, 8, ROW), axis=0)
                out_t = out_t + dot(vx[h, pl.ds(start, ROW), :], e.astype(BF16), TN)
            return total, out_t

        total, out_t = lax.fori_loop(
            0, 3, second, (jnp.zeros((8, ROW), F32), jnp.zeros((HD, ROW), F32))
        )
        inverse = 1.0 / jnp.sum(total, axis=0, keepdims=True)
        out = jnp.transpose(out_t * inverse).astype(BF16)
        o_st[h, base : base + ROW, :] = out
        products = jnp.transpose(out.astype(F32) * c.astype(F32))
        grad_dot = jnp.sum(products, axis=0, keepdims=True)
        inverse_scaled = inverse * scale

        def third(f, gq_t):
            for n in near:
                start = pl.multiple_of(f * FRAME + n * ROW, ROW)
                here = pl.ds(start, ROW)
                e = s_buf[here, :]
                gp = dot(vx[h, here, :], c, NT)
                p_low = (e * inverse).astype(BF16)
                gs = ((e * inverse_scaled) * (gp - grad_dot)).astype(BF16)
                gv = dot(p_low, c, NN)
                gk = dot(gs, q, NN)
                if r == max(n - 1, 0):
                    gv_acc[here, :] = gv
                    gk_acc[here, :] = gk
                else:
                    gv_acc[here, :] += gv
                    gk_acc[here, :] += gk
                gq_t = gq_t + dot(kx[h, here, :], gs, TN)
            return gq_t

        gq_t = lax.fori_loop(0, 3, third, jnp.zeros((HD, ROW), F32))
        gq_st[h, base : base + ROW, :] = jnp.transpose(gq_t).astype(BF16)

    def send_out(a, h):
        for peer in peers:
            out_copy(a, h, peer, z).start()
        out_local(a, h).start()

    def finish(h):
        for side, there in ((1, has_prev), (0, has_next)):
            @pl.when(there)
            def _(side=side):
                for a in range(2):
                    grad_copy(a, h, side).wait_recv()
                    acc = (gk_acc, gv_acc)[a]
                    acc[FRAME : 2 * FRAME, :] += g_in[a, h, side].astype(F32)
        for a in range(2):
            stages[2 + a][h] = (gk_acc, gv_acc)[a][FRAME : 2 * FRAME, :].astype(BF16)
            send_out(2 + a, h)

    forward(0)

    def one_head(h, _):
        wait_in(h, (2, 3))
        for side, there in ((0, has_prev), (1, has_next)):
            @pl.when(there)
            def _(side=side):
                for a in range(2):
                    halo_copy(a, h, side).wait_recv()

        @pl.when(h > 0)
        def _():
            finish(h - 1)

        for r in range(TILE_ROWS):
            attend(h, r)
        for side, there in ((0, has_prev), (1, has_next)):
            @pl.when(there)
            def _(side=side):
                for a in range(2):
                    part = (gk_acc, gv_acc)[a][pl.ds(2 * FRAME * side, FRAME), :]
                    g_out[a, h, side] = part.astype(BF16)
                    grad_copy(a, h, side).start()
        send_out(0, h)
        send_out(1, h)

        @pl.when(h + 1 < heads)
        def _():
            forward(h + 1)

        return 0

    lax.fori_loop(0, heads, one_head, 0)
    finish(heads - 1)

    def drain(h, _):
        for a in range(4):
            for peer in peers:
                in_copy(a, h, peer, z).wait_send()
                out_copy(a, h, peer, z).wait_send()
                out_copy(a, h, peer, peer).wait_recv()
            out_local(a, h).wait()
        for a in range(2):
            for side, there, back in ((0, has_next, has_prev), (1, has_prev, has_next)):
                @pl.when(there)
                def _(a=a, side=side):
                    halo_copy(a, h, side).wait_send()

                @pl.when(back)
                def _(a=a, side=side):
                    grad_copy(a, h, side).wait_send()
        return 0

    lax.fori_loop(0, heads, drain, 0)


def shards(nseq, nz, queries, keys, values, cotangent, neighbours):
    rows, width = queries.shape
    heads = width // HD // nz
    first_tile = lax.axis_index("seq") * TILES_F
    listed = lax.dynamic_slice_in_dim(neighbours, first_tile, TILES_F, 0)
    relative = jnp.where(listed >= 0, listed - (first_tile - TILES_F), -1)
    near = jnp.arange(3 * TILES_F, dtype=jnp.int32)
    present = jnp.any(relative[:, :, None] == near[None, None, :], axis=1)
    bias = jnp.where(present, 0.0, masked_score).astype(F32)
    bias = bias.reshape(TILE_ROWS, TILE_COLS, 3 * TILE_ROWS, TILE_COLS).transpose(0, 2, 3, 1)
    bias = jnp.repeat(bias, TILE, axis=3)
    bias = jnp.pad(bias, ((0, 0), (0, 0), (0, 8 - TILE_COLS), (0, 0)))
    vmem = pl.BlockSpec(memory_space=pltpu.VMEM)
    dma = pltpu.SemaphoreType.DMA
    return pl.pallas_call(
        functools.partial(kernel, nseq, nz, heads, rows),
        out_shape=[jax.ShapeDtypeStruct((rows, width), BF16)] * 4,
        in_specs=[vmem] * 5,
        out_specs=[vmem] * 4,
        scratch_shapes=[
            pltpu.VMEM((heads, 3 * FRAME, HD), BF16),
            pltpu.VMEM((heads, 3 * FRAME, HD), BF16),
            pltpu.VMEM((heads, FRAME, HD), BF16),
            pltpu.VMEM((heads, FRAME, HD), BF16),
            pltpu.VMEM((heads, FRAME, HD), BF16),
            pltpu.VMEM((heads, FRAME, HD), BF16),
            pltpu.VMEM((heads, FRAME, HD), BF16),
            pltpu.VMEM((heads, FRAME, HD), BF16),
            pltpu.VMEM((2, heads, 2, FRAME, HD), BF16),
            pltpu.VMEM((2, heads, 2, FRAME, HD), BF16),
            pltpu.VMEM((3 * FRAME, ROW), F32),
            pltpu.VMEM((3 * FRAME, HD), F32),
            pltpu.VMEM((3 * FRAME, HD), F32),
            dma((4, heads, nz)),
            dma((4, heads, nz)),
            dma((4, heads)),
            dma((2, heads, 2)),
            dma((2, heads, 2)),
            dma((2, heads, 2)),
            dma((2, heads, 2)),
            dma((4, heads, nz)),
            dma((4, heads, nz)),
            dma((4, heads)),
        ],
        compiler_params=pltpu.CompilerParams(
            collective_id=0, has_side_effects=True, vmem_limit_bytes=56 * 1024 * 1024
        ),
    )(keys, values, queries, cotangent, bias)


def solution(mesh):
    placed = P(("seq", "head"), None)
    return jax.shard_map(
        functools.partial(shards, mesh.shape["seq"], mesh.shape["head"]),
        mesh=mesh,
        in_specs=(placed, placed, placed, placed, P()),
        out_specs=(placed, placed, placed, placed),
        check_vma=False,
    )
```

```python
import functools
import math

import jax
import jax.numpy as jnp
from jax import lax
from jax.experimental import pallas as pl
from jax.experimental.pallas import tpu as pltpu
from jax.sharding import PartitionSpec as P

TILE = 64
TILE_ROWS = 3
TILE_COLS = 4
TILES_F = 12
HD = 128
FRAME = TILE * TILES_F
ROW = TILE * TILE_COLS
MESH = pl.DeviceIdType.MESH
masked_score = -1e30
F32 = jnp.float32
BF16 = jnp.bfloat16

NT = (((1,), (1,)), ((), ()))
TN = (((0,), (0,)), ((), ()))
NN = (((1,), (0,)), ((), ()))


def dot(a, b, dims):
    return lax.dot_general(a, b, dims, preferred_element_type=F32)


def kernel(
    nseq, nz, heads, rows,
    k_in, v_in, q_in, c_in, near_ref,
    o_out, gq_out, gk_out, gv_out,
    kx, vx, qb, cb, o_st, gq_st, gk_st, gv_st, g_out, g_in, s_buf, gk_acc, gv_acc, bias_ref,
    in_send, in_recv, in_loc, halo_send, halo_recv, g_send, g_recv, out_send, out_recv, out_loc,
):
    s = lax.axis_index("seq")
    z = lax.axis_index("head")
    has_prev = s > 0
    has_next = s < nseq - 1
    scale = 1.0 / math.sqrt(HD)
    log2_scale = scale * math.log2(math.e)

    peers = [lax.rem(z + d, nz) for d in range(1, nz)]
    ins = (k_in, v_in, q_in, c_in)
    outs = (o_out, gq_out, gk_out, gv_out)
    stages = (o_st, gq_st, gk_st, gv_st)

    def in_place(a, h, source):
        if a < 2:
            start = FRAME + source * rows
            return (kx, vx)[a].at[h, pl.ds(pl.multiple_of(start, 32), rows), :]
        return (qb, cb)[a - 2].at[h, pl.ds(pl.multiple_of(source * rows, 32), rows), :]

    def columns(owner, h):
        return pl.ds(pl.multiple_of((owner * heads + h) * HD, HD), HD)

    def in_copy(a, h, peer, source):
        return pltpu.make_async_remote_copy(
            src_ref=ins[a].at[:, columns(peer, h)],
            dst_ref=in_place(a, h, source),
            send_sem=in_send.at[a, h, peer],
            recv_sem=in_recv.at[a, h, source],
            device_id=(s, peer),
            device_id_type=MESH,
        )

    def in_local(a, h):
        return pltpu.make_async_copy(
            ins[a].at[:, columns(z, h)], in_place(a, h, z), in_loc.at[a, h]
        )

    def out_copy(a, h, peer, source):
        return pltpu.make_async_remote_copy(
            src_ref=stages[a].at[h, pl.ds(pl.multiple_of(peer * rows, 32), rows), :],
            dst_ref=outs[a].at[:, columns(source, h)],
            send_sem=out_send.at[a, h, peer],
            recv_sem=out_recv.at[a, h, source],
            device_id=(s, peer),
            device_id_type=MESH,
        )

    def out_local(a, h):
        return pltpu.make_async_copy(
            stages[a].at[h, pl.ds(pl.multiple_of(z * rows, 32), rows), :],
            outs[a].at[:, columns(z, h)],
            out_loc.at[a, h],
        )

    def halo_copy(a, h, side):
        ext = (kx, vx)[a]
        return pltpu.make_async_remote_copy(
            src_ref=ext.at[h, pl.ds(FRAME, FRAME), :],
            dst_ref=ext.at[h, pl.ds(2 * FRAME * side, FRAME), :],
            send_sem=halo_send.at[a, h, side],
            recv_sem=halo_recv.at[a, h, side],
            device_id=(s + 1 - 2 * side, z),
            device_id_type=MESH,
        )

    def grad_copy(a, h, side):
        return pltpu.make_async_remote_copy(
            src_ref=g_out.at[a, h, side],
            dst_ref=g_in.at[a, h, side],
            send_sem=g_send.at[a, h, side],
            recv_sem=g_recv.at[a, h, side],
            device_id=(s - 1 + 2 * side, z),
            device_id_type=MESH,
        )

    barrier = pltpu.get_barrier_semaphore()
    for peer in peers:
        pl.semaphore_signal(barrier, inc=1, device_id=(s, peer), device_id_type=MESH)

    @pl.when(has_prev)
    def _():
        pl.semaphore_signal(barrier, inc=1, device_id=(s - 1, z), device_id_type=MESH)

    @pl.when(has_next)
    def _():
        pl.semaphore_signal(barrier, inc=1, device_id=(s + 1, z), device_id_type=MESH)

    pl.semaphore_wait(barrier, nz - 1 + has_prev.astype(jnp.int32) + has_next.astype(jnp.int32))

    def start_in(h, _):
        for a in range(4):
            for peer in peers:
                in_copy(a, h, peer, z).start()
            in_local(a, h).start()
        return 0

    lax.fori_loop(0, heads, start_in, 0)

    first_tile = s * TILES_F
    ext_rows = 40
    listed = near_ref[...]
    count = listed.shape[1]
    ext_row = lax.broadcasted_iota(jnp.int32, (ext_rows, count), 0)
    present = jnp.zeros((ext_rows, count), F32)
    for k in range(3 * TILES_F):
        tile = first_tile - TILES_F + k
        match = (listed == tile) & (listed >= 0)
        match = jnp.max(jnp.where(match, 1.0, 0.0).astype(F32), axis=0, keepdims=True)
        present = jnp.where(ext_row == k, match, present)
    present = present.astype(BF16)
    tile_row = lax.broadcasted_iota(jnp.int32, (count, ROW), 0)
    lane_tile = first_tile + lax.broadcasted_iota(jnp.int32, (count, ROW), 1) // TILE
    for r in range(TILE_ROWS):
        spread = jnp.where(tile_row == lane_tile + r * TILE_COLS, 1.0, 0.0).astype(BF16)
        bias = jnp.where(dot(present, spread, NN) > 0.5, 0.0, masked_score).astype(F32)
        for n in range(3 * TILE_ROWS):
            bias_ref[r, n, 0:TILE_COLS, :] = bias[n * TILE_COLS : (n + 1) * TILE_COLS, :]

    @pl.when(jnp.logical_not(has_prev))
    def _():
        kx[:, 0:FRAME, :] = jnp.zeros((heads, FRAME, HD), BF16)
        vx[:, 0:FRAME, :] = jnp.zeros((heads, FRAME, HD), BF16)

    @pl.when(jnp.logical_not(has_next))
    def _():
        kx[:, 2 * FRAME : 3 * FRAME, :] = jnp.zeros((heads, FRAME, HD), BF16)
        vx[:, 2 * FRAME : 3 * FRAME, :] = jnp.zeros((heads, FRAME, HD), BF16)

    def wait_in(h, arrays):
        for a in arrays:
            for peer in peers:
                in_copy(a, h, peer, peer).wait_recv()
            in_local(a, h).wait()

    def forward(h):
        wait_in(h, (0, 1))
        for side, there in ((0, has_next), (1, has_prev)):
            @pl.when(there)
            def _(side=side):
                for a in range(2):
                    halo_copy(a, h, side).start()

    def attend(h, r):
        low, high = max(r - 1, 0), min(r + 1, TILE_ROWS - 1)
        near = range(low, high + 1)
        base = r * ROW
        q = qb[h, base : base + ROW, :]
        c = cb[h, base : base + ROW, :]

        def first(f, top):
            for n in near:
                start = pl.multiple_of(f * FRAME + n * ROW, ROW)
                t = dot(kx[h, pl.ds(start, ROW), :], q, NT) * log2_scale
                rows_bias = bias_ref[r, f * TILE_ROWS + n]
                parts = []
                for k in range(TILE_COLS):
                    part = t[k * TILE : (k + 1) * TILE, :] + rows_bias[k : k + 1, :]
                    s_buf[pl.ds(start + k * TILE, TILE), :] = part
                    top = jnp.maximum(top, jnp.max(part.reshape(TILE // 8, 8, ROW), axis=0))
            return top

        top = lax.fori_loop(0, 3, first, jnp.full((8, ROW), masked_score, F32))
        top = jnp.max(top, axis=0, keepdims=True)

        def second(f, carry):
            total, out_t = carry
            for n in near:
                start = pl.multiple_of(f * FRAME + n * ROW, ROW)
                e = jnp.exp2(s_buf[pl.ds(start, ROW), :] - top)
                s_buf[pl.ds(start, ROW), :] = e
                total = total + jnp.sum(e.reshape(ROW // 8, 8, ROW), axis=0)
                out_t = out_t + dot(vx[h, pl.ds(start, ROW), :], e.astype(BF16), TN)
            return total, out_t

        total, out_t = lax.fori_loop(
            0, 3, second, (jnp.zeros((8, ROW), F32), jnp.zeros((HD, ROW), F32))
        )
        inverse = 1.0 / jnp.sum(total, axis=0, keepdims=True)
        out = jnp.transpose(out_t * inverse).astype(BF16)
        o_st[h, base : base + ROW, :] = out
        products = jnp.transpose(out.astype(F32) * c.astype(F32))
        grad_dot = jnp.sum(products, axis=0, keepdims=True)
        inverse_scaled = inverse * scale

        def third(f, gq_t):
            for n in near:
                start = pl.multiple_of(f * FRAME + n * ROW, ROW)
                here = pl.ds(start, ROW)
                e = s_buf[here, :]
                gp = dot(vx[h, here, :], c, NT)
                p_low = (e * inverse).astype(BF16)
                gs = ((e * inverse_scaled) * (gp - grad_dot)).astype(BF16)
                gv = dot(p_low, c, NN)
                gk = dot(gs, q, NN)
                if r == max(n - 1, 0):
                    gv_acc[here, :] = gv
                    gk_acc[here, :] = gk
                else:
                    gv_acc[here, :] += gv
                    gk_acc[here, :] += gk
                gq_t = gq_t + dot(kx[h, here, :], gs, TN)
            return gq_t

        gq_t = lax.fori_loop(0, 3, third, jnp.zeros((HD, ROW), F32))
        gq_st[h, base : base + ROW, :] = jnp.transpose(gq_t).astype(BF16)

    def send_out(a, h):
        for peer in peers:
            out_copy(a, h, peer, z).start()
        out_local(a, h).start()

    def finish(h):
        for side, there in ((1, has_prev), (0, has_next)):
            @pl.when(there)
            def _(side=side):
                for a in range(2):
                    grad_copy(a, h, side).wait_recv()
                    acc = (gk_acc, gv_acc)[a]
                    acc[FRAME : 2 * FRAME, :] += g_in[a, h, side].astype(F32)
        for a in range(2):
            stages[2 + a][h] = (gk_acc, gv_acc)[a][FRAME : 2 * FRAME, :].astype(BF16)

    forward(0)

    def one_head(h, _):
        wait_in(h, (2, 3))
        for side, there in ((0, has_prev), (1, has_next)):
            @pl.when(there)
            def _(side=side):
                for a in range(2):
                    halo_copy(a, h, side).wait_recv()

        @pl.when(h > 0)
        def _():
            finish(h - 1)

        @pl.when((h > 0) & (h == heads - 1))
        def _():
            send_out(2, h - 1)
            send_out(3, h - 1)

        for r in range(TILE_ROWS):
            attend(h, r)
        for side, there in ((0, has_prev), (1, has_next)):
            @pl.when(there)
            def _(side=side):
                for a in range(2):
                    part = (gk_acc, gv_acc)[a][pl.ds(2 * FRAME * side, FRAME), :]
                    g_out[a, h, side] = part.astype(BF16)
                    grad_copy(a, h, side).start()

        @pl.when(h == heads - 1)
        def _():
            send_out(0, h)
            send_out(1, h)

        @pl.when(h + 1 < heads)
        def _():
            forward(h + 1)

        @pl.when(h == heads - 2)
        def _():
            def flush(ready, _):
                send_out(0, ready)
                send_out(1, ready)

                @pl.when(ready < heads - 2)
                def _():
                    send_out(2, ready)
                    send_out(3, ready)

                return 0

            lax.fori_loop(0, heads - 1, flush, 0)

        return 0

    lax.fori_loop(0, heads, one_head, 0)
    finish(heads - 1)
    send_out(2, heads - 1)
    send_out(3, heads - 1)

    def drain(h, _):
        for a in range(4):
            for peer in peers:
                in_copy(a, h, peer, z).wait_send()
                out_copy(a, h, peer, z).wait_send()
                out_copy(a, h, peer, peer).wait_recv()
            out_local(a, h).wait()
        for a in range(2):
            for side, there, back in ((0, has_next, has_prev), (1, has_prev, has_next)):
                @pl.when(there)
                def _(a=a, side=side):
                    halo_copy(a, h, side).wait_send()

                @pl.when(back)
                def _(a=a, side=side):
                    grad_copy(a, h, side).wait_send()
        return 0

    lax.fori_loop(0, heads, drain, 0)


def place_results(*refs):
    done = refs[8]
    copies = [pltpu.make_async_copy(refs[a], refs[4 + a], done.at[a]) for a in range(4)]
    for copy in copies:
        copy.start()
    for copy in copies:
        copy.wait()


def shards(nseq, nz, queries, keys, values, cotangent, neighbours):
    rows, width = queries.shape
    heads = width // HD // nz
    place = pl.BlockSpec(memory_space=pl.ANY)
    dma = pltpu.SemaphoreType.DMA
    results = pl.pallas_call(
        functools.partial(kernel, nseq, nz, heads, rows),
        out_shape=[jax.ShapeDtypeStruct((rows, width), BF16)] * 4,
        in_specs=[place] * 4 + [pl.BlockSpec(memory_space=pltpu.VMEM)],
        out_specs=[place] * 4,
        scratch_shapes=[
            pltpu.VMEM((heads, 3 * FRAME, HD), BF16),
            pltpu.VMEM((heads, 3 * FRAME, HD), BF16),
            pltpu.VMEM((heads, FRAME, HD), BF16),
            pltpu.VMEM((heads, FRAME, HD), BF16),
            pltpu.VMEM((heads, FRAME, HD), BF16),
            pltpu.VMEM((heads, FRAME, HD), BF16),
            pltpu.VMEM((heads, FRAME, HD), BF16),
            pltpu.VMEM((heads, FRAME, HD), BF16),
            pltpu.VMEM((2, heads, 2, FRAME, HD), BF16),
            pltpu.VMEM((2, heads, 2, FRAME, HD), BF16),
            pltpu.VMEM((3 * FRAME, ROW), F32),
            pltpu.VMEM((3 * FRAME, HD), F32),
            pltpu.VMEM((3 * FRAME, HD), F32),
            pltpu.VMEM((TILE_ROWS, 3 * TILE_ROWS, 8, ROW), F32),
            dma((4, heads, nz)),
            dma((4, heads, nz)),
            dma((4, heads)),
            dma((2, heads, 2)),
            dma((2, heads, 2)),
            dma((2, heads, 2)),
            dma((2, heads, 2)),
            dma((4, heads, nz)),
            dma((4, heads, nz)),
            dma((4, heads)),
        ],
        compiler_params=pltpu.CompilerParams(
            collective_id=0, has_side_effects=True, vmem_limit_bytes=56 * 1024 * 1024
        ),
    )(keys, values, queries, cotangent, neighbours.T)
    return pl.pallas_call(
        place_results,
        out_shape=[jax.ShapeDtypeStruct((rows, width), BF16)] * 4,
        in_specs=[place] * 4,
        out_specs=[place] * 4,
        scratch_shapes=[dma((4,))],
        compiler_params=pltpu.CompilerParams(vmem_limit_bytes=56 * 1024 * 1024),
    )(*results)


def solution(mesh):
    placed = P(("seq", "head"), None)
    return jax.shard_map(
        functools.partial(shards, mesh.shape["seq"], mesh.shape["head"]),
        mesh=mesh,
        in_specs=(placed, placed, placed, placed, P()),
        out_specs=(placed, placed, placed, placed),
        check_vma=False,
    )
```

```python
import functools
import math

import jax
import jax.numpy as jnp
from jax import lax
from jax.experimental import pallas as pl
from jax.experimental.pallas import tpu as pltpu
from jax.sharding import PartitionSpec as P

TILE = 64
TILE_ROWS = 3
TILE_COLS = 4
TILES_F = 12
HD = 128
FRAME = TILE * TILES_F
ROW = TILE * TILE_COLS
MESH = pl.DeviceIdType.MESH
masked_score = -1e30
F32 = jnp.float32
BF16 = jnp.bfloat16

NT = (((1,), (1,)), ((), ()))
TN = (((0,), (0,)), ((), ()))
NN = (((1,), (0,)), ((), ()))


def dot(a, b, dims):
    return lax.dot_general(a, b, dims, preferred_element_type=F32)


def kernel(
    nseq, nz, heads, rows,
    k_in, v_in, q_in, c_in, near_ref,
    o_out, gq_out, gk_out, gv_out,
    kx, vx, qb, cb, o_st, gq_st, gk_st, gv_st, g_out, g_in, s_buf, gk_acc, gv_acc, bias_ref,
    in_send, in_recv, in_loc, halo_send, halo_recv, g_send, g_recv, out_send, out_recv, out_loc,
):
    s = lax.axis_index("seq")
    z = lax.axis_index("head")
    has_prev = s > 0
    has_next = s < nseq - 1
    scale = 1.0 / math.sqrt(HD)
    log2_scale = scale * math.log2(math.e)

    peers = [lax.rem(z + d, nz) for d in range(1, nz)]
    ins = (k_in, v_in, q_in, c_in)
    outs = (o_out, gq_out, gk_out, gv_out)
    stages = (o_st, gq_st, gk_st, gv_st)

    def in_place(a, h, source):
        if a < 2:
            start = FRAME + source * rows
            return (kx, vx)[a].at[h, pl.ds(pl.multiple_of(start, 32), rows), :]
        return (qb, cb)[a - 2].at[h, pl.ds(pl.multiple_of(source * rows, 32), rows), :]

    def columns(owner, h):
        return pl.ds(pl.multiple_of((owner * heads + h) * HD, HD), HD)

    def in_copy(a, h, peer, source):
        return pltpu.make_async_remote_copy(
            src_ref=ins[a].at[:, columns(peer, h)],
            dst_ref=in_place(a, h, source),
            send_sem=in_send.at[a, h, peer],
            recv_sem=in_recv.at[a, h, source],
            device_id=(s, peer),
            device_id_type=MESH,
        )

    def in_local(a, h):
        return pltpu.make_async_copy(
            ins[a].at[:, columns(z, h)], in_place(a, h, z), in_loc.at[a, h]
        )

    def out_copy(a, h, peer, source):
        return pltpu.make_async_remote_copy(
            src_ref=stages[a].at[h, pl.ds(pl.multiple_of(peer * rows, 32), rows), :],
            dst_ref=outs[a].at[:, columns(source, h)],
            send_sem=out_send.at[a, h, peer],
            recv_sem=out_recv.at[a, h, source],
            device_id=(s, peer),
            device_id_type=MESH,
        )

    def out_local(a, h):
        return pltpu.make_async_copy(
            stages[a].at[h, pl.ds(pl.multiple_of(z * rows, 32), rows), :],
            outs[a].at[:, columns(z, h)],
            out_loc.at[a, h],
        )

    def halo_copy(a, h, side):
        ext = (kx, vx)[a]
        return pltpu.make_async_remote_copy(
            src_ref=ext.at[h, pl.ds(FRAME, FRAME), :],
            dst_ref=ext.at[h, pl.ds(2 * FRAME * side, FRAME), :],
            send_sem=halo_send.at[a, h, side],
            recv_sem=halo_recv.at[a, h, side],
            device_id=(s + 1 - 2 * side, z),
            device_id_type=MESH,
        )

    def grad_copy(a, h, side):
        return pltpu.make_async_remote_copy(
            src_ref=g_out.at[a, h, side],
            dst_ref=g_in.at[a, h, side],
            send_sem=g_send.at[a, h, side],
            recv_sem=g_recv.at[a, h, side],
            device_id=(s - 1 + 2 * side, z),
            device_id_type=MESH,
        )

    barrier = pltpu.get_barrier_semaphore()
    for peer in peers:
        pl.semaphore_signal(barrier, inc=1, device_id=(s, peer), device_id_type=MESH)

    @pl.when(has_prev)
    def _():
        pl.semaphore_signal(barrier, inc=1, device_id=(s - 1, z), device_id_type=MESH)

    @pl.when(has_next)
    def _():
        pl.semaphore_signal(barrier, inc=1, device_id=(s + 1, z), device_id_type=MESH)

    pl.semaphore_wait(barrier, nz - 1 + has_prev.astype(jnp.int32) + has_next.astype(jnp.int32))

    def start_in(h, _):
        for a in range(4):
            for peer in peers:
                in_copy(a, h, peer, z).start()
            in_local(a, h).start()
        return 0

    lax.fori_loop(0, heads, start_in, 0)

    first_tile = s * TILES_F
    ext_rows = 40
    listed = near_ref[...]
    count = listed.shape[1]
    ext_row = lax.broadcasted_iota(jnp.int32, (ext_rows, count), 0)
    present = jnp.zeros((ext_rows, count), F32)
    for k in range(3 * TILES_F):
        tile = first_tile - TILES_F + k
        match = (listed == tile) & (listed >= 0)
        match = jnp.max(jnp.where(match, 1.0, 0.0).astype(F32), axis=0, keepdims=True)
        present = jnp.where(ext_row == k, match, present)
    present = present.astype(BF16)
    tile_row = lax.broadcasted_iota(jnp.int32, (count, ROW), 0)
    lane_tile = first_tile + lax.broadcasted_iota(jnp.int32, (count, ROW), 1) // TILE
    for r in range(TILE_ROWS):
        spread = jnp.where(tile_row == lane_tile + r * TILE_COLS, 1.0, 0.0).astype(BF16)
        bias = jnp.where(dot(present, spread, NN) > 0.5, 0.0, masked_score).astype(F32)
        for n in range(3 * TILE_ROWS):
            bias_ref[r, n, 0:TILE_COLS, :] = bias[n * TILE_COLS : (n + 1) * TILE_COLS, :]

    @pl.when(jnp.logical_not(has_prev))
    def _():
        kx[:, 0:FRAME, :] = jnp.zeros((heads, FRAME, HD), BF16)
        vx[:, 0:FRAME, :] = jnp.zeros((heads, FRAME, HD), BF16)

    @pl.when(jnp.logical_not(has_next))
    def _():
        kx[:, 2 * FRAME : 3 * FRAME, :] = jnp.zeros((heads, FRAME, HD), BF16)
        vx[:, 2 * FRAME : 3 * FRAME, :] = jnp.zeros((heads, FRAME, HD), BF16)

    def wait_in(h, arrays):
        for a in arrays:
            for peer in peers:
                in_copy(a, h, peer, peer).wait_recv()
            in_local(a, h).wait()

    def forward(h):
        wait_in(h, (0, 1))
        for side, there in ((0, has_next), (1, has_prev)):
            @pl.when(there)
            def _(side=side):
                for a in range(2):
                    halo_copy(a, h, side).start()

    def attend(h, r):
        low, high = max(r - 1, 0), min(r + 1, TILE_ROWS - 1)
        near = range(low, high + 1)
        base = r * ROW
        q = qb[h, base : base + ROW, :]
        c = cb[h, base : base + ROW, :]

        def first(f, top):
            for n in near:
                start = pl.multiple_of(f * FRAME + n * ROW, ROW)
                t = dot(kx[h, pl.ds(start, ROW), :], q, NT) * log2_scale
                rows_bias = bias_ref[r, f * TILE_ROWS + n]
                parts = []
                for k in range(TILE_COLS):
                    part = t[k * TILE : (k + 1) * TILE, :] + rows_bias[k : k + 1, :]
                    s_buf[pl.ds(start + k * TILE, TILE), :] = part
                    top = jnp.maximum(top, jnp.max(part.reshape(TILE // 8, 8, ROW), axis=0))
            return top

        top = lax.fori_loop(0, 3, first, jnp.full((8, ROW), masked_score, F32))
        top = jnp.max(top, axis=0, keepdims=True)

        def second(f, carry):
            total, out_t = carry
            for n in near:
                start = pl.multiple_of(f * FRAME + n * ROW, ROW)
                e = jnp.exp2(s_buf[pl.ds(start, ROW), :] - top)
                s_buf[pl.ds(start, ROW), :] = e
                total = total + jnp.sum(e.reshape(ROW // 8, 8, ROW), axis=0)
                out_t = out_t + dot(vx[h, pl.ds(start, ROW), :], e.astype(BF16), TN)
            return total, out_t

        total, out_t = lax.fori_loop(
            0, 3, second, (jnp.zeros((8, ROW), F32), jnp.zeros((HD, ROW), F32))
        )
        inverse = 1.0 / jnp.sum(total, axis=0, keepdims=True)
        out = jnp.transpose(out_t * inverse).astype(BF16)
        o_st[h, base : base + ROW, :] = out
        products = jnp.transpose(out.astype(F32) * c.astype(F32))
        grad_dot = jnp.sum(products, axis=0, keepdims=True)
        inverse_scaled = inverse * scale

        def third(f, gq_t):
            for n in near:
                start = pl.multiple_of(f * FRAME + n * ROW, ROW)
                here = pl.ds(start, ROW)
                e = s_buf[here, :]
                gp = dot(vx[h, here, :], c, NT)
                p_low = (e * inverse).astype(BF16)
                gs = ((e * inverse_scaled) * (gp - grad_dot)).astype(BF16)
                gv = dot(p_low, c, NN)
                gk = dot(gs, q, NN)
                if r == max(n - 1, 0):
                    gv_acc[here, :] = gv
                    gk_acc[here, :] = gk
                else:
                    gv_acc[here, :] += gv
                    gk_acc[here, :] += gk
                gq_t = gq_t + dot(kx[h, here, :], gs, TN)
            return gq_t

        gq_t = lax.fori_loop(0, 3, third, jnp.zeros((HD, ROW), F32))
        gq_st[h, base : base + ROW, :] = jnp.transpose(gq_t).astype(BF16)

    def send_out(a, h):
        for peer in peers:
            out_copy(a, h, peer, z).start()
        out_local(a, h).start()

    def finish(h):
        for side, there in ((1, has_prev), (0, has_next)):
            @pl.when(there)
            def _(side=side):
                for a in range(2):
                    grad_copy(a, h, side).wait_recv()
                    acc = (gk_acc, gv_acc)[a]
                    acc[FRAME : 2 * FRAME, :] += g_in[a, h, side].astype(F32)
        for a in range(2):
            stages[2 + a][h] = (gk_acc, gv_acc)[a][FRAME : 2 * FRAME, :].astype(BF16)

    forward(0)

    def one_head(h, _):
        wait_in(h, (2, 3))
        for side, there in ((0, has_prev), (1, has_next)):
            @pl.when(there)
            def _(side=side):
                for a in range(2):
                    halo_copy(a, h, side).wait_recv()

        @pl.when(h > 0)
        def _():
            finish(h - 1)

        @pl.when((h > 0) & (h == heads - 1))
        def _():
            send_out(2, h - 1)
            send_out(3, h - 1)

        for r in range(TILE_ROWS):
            attend(h, r)
        for side, there in ((0, has_prev), (1, has_next)):
            @pl.when(there)
            def _(side=side):
                for a in range(2):
                    part = (gk_acc, gv_acc)[a][pl.ds(2 * FRAME * side, FRAME), :]
                    g_out[a, h, side] = part.astype(BF16)
                    grad_copy(a, h, side).start()

        @pl.when(h == heads - 1)
        def _():
            send_out(0, h)
            send_out(1, h)

        @pl.when(h + 1 < heads)
        def _():
            forward(h + 1)

        @pl.when(h == heads - 2)
        def _():
            def flush(ready, _):
                send_out(0, ready)
                send_out(1, ready)

                @pl.when(ready < heads - 2)
                def _():
                    send_out(2, ready)
                    send_out(3, ready)

                return 0

            lax.fori_loop(0, heads - 1, flush, 0)

        return 0

    lax.fori_loop(0, heads, one_head, 0)
    finish(heads - 1)
    send_out(2, heads - 1)
    send_out(3, heads - 1)

    def drain(h, _):
        for a in range(4):
            for peer in peers:
                in_copy(a, h, peer, z).wait_send()
                out_copy(a, h, peer, z).wait_send()
                out_copy(a, h, peer, peer).wait_recv()
            out_local(a, h).wait()
        for a in range(2):
            for side, there, back in ((0, has_next, has_prev), (1, has_prev, has_next)):
                @pl.when(there)
                def _(a=a, side=side):
                    halo_copy(a, h, side).wait_send()

                @pl.when(back)
                def _(a=a, side=side):
                    grad_copy(a, h, side).wait_send()
        return 0

    lax.fori_loop(0, heads, drain, 0)


def place_results(*refs):
    for a in range(4):
        refs[4 + a][...] = refs[a][...]


def shards(nseq, nz, queries, keys, values, cotangent, neighbours):
    rows, width = queries.shape
    heads = width // HD // nz
    vmem = pl.BlockSpec(memory_space=pltpu.VMEM)
    dma = pltpu.SemaphoreType.DMA
    results = pl.pallas_call(
        functools.partial(kernel, nseq, nz, heads, rows),
        out_shape=[jax.ShapeDtypeStruct((rows, width), BF16)] * 4,
        in_specs=[vmem] * 5,
        out_specs=[vmem] * 4,
        scratch_shapes=[
            pltpu.VMEM((heads, 3 * FRAME, HD), BF16),
            pltpu.VMEM((heads, 3 * FRAME, HD), BF16),
            pltpu.VMEM((heads, FRAME, HD), BF16),
            pltpu.VMEM((heads, FRAME, HD), BF16),
            pltpu.VMEM((heads, FRAME, HD), BF16),
            pltpu.VMEM((heads, FRAME, HD), BF16),
            pltpu.VMEM((heads, FRAME, HD), BF16),
            pltpu.VMEM((heads, FRAME, HD), BF16),
            pltpu.VMEM((2, heads, 2, FRAME, HD), BF16),
            pltpu.VMEM((2, heads, 2, FRAME, HD), BF16),
            pltpu.VMEM((3 * FRAME, ROW), F32),
            pltpu.VMEM((3 * FRAME, HD), F32),
            pltpu.VMEM((3 * FRAME, HD), F32),
            pltpu.VMEM((TILE_ROWS, 3 * TILE_ROWS, 8, ROW), F32),
            dma((4, heads, nz)),
            dma((4, heads, nz)),
            dma((4, heads)),
            dma((2, heads, 2)),
            dma((2, heads, 2)),
            dma((2, heads, 2)),
            dma((2, heads, 2)),
            dma((4, heads, nz)),
            dma((4, heads, nz)),
            dma((4, heads)),
        ],
        compiler_params=pltpu.CompilerParams(
            collective_id=0, has_side_effects=True, vmem_limit_bytes=56 * 1024 * 1024
        ),
    )(keys, values, queries, cotangent, neighbours.T)
    block_rows = 48 if rows % 48 == 0 else rows
    block = pl.BlockSpec((block_rows, width), lambda i: (i, 0))
    return pl.pallas_call(
        place_results,
        grid=(rows // block_rows,),
        out_shape=[jax.ShapeDtypeStruct((rows, width), BF16)] * 4,
        in_specs=[block] * 4,
        out_specs=[block] * 4,
        compiler_params=pltpu.CompilerParams(vmem_limit_bytes=56 * 1024 * 1024),
    )(*results)


def solution(mesh):
    placed = P(("seq", "head"), None)
    return jax.shard_map(
        functools.partial(shards, mesh.shape["seq"], mesh.shape["head"]),
        mesh=mesh,
        in_specs=(placed, placed, placed, placed, P()),
        out_specs=(placed, placed, placed, placed),
        check_vma=False,
    )
```

```python
import functools
import math

import jax
import jax.numpy as jnp
from jax import lax
from jax.experimental import pallas as pl
from jax.experimental.pallas import tpu as pltpu
from jax.sharding import PartitionSpec as P

TILE = 64
TILE_ROWS = 3
TILE_COLS = 4
TILES_F = 12
HD = 128
FRAME = TILE * TILES_F
ROW = TILE * TILE_COLS
MESH = pl.DeviceIdType.MESH
masked_score = -1e30
F32 = jnp.float32
BF16 = jnp.bfloat16

NT = (((1,), (1,)), ((), ()))
TN = (((0,), (0,)), ((), ()))
NN = (((1,), (0,)), ((), ()))


def dot(a, b, dims):
    return lax.dot_general(a, b, dims, preferred_element_type=F32)


def kernel(
    nseq, nz, heads, rows,
    k_in, v_in, q_in, c_in, near_ref,
    o_out, gq_out, gk_out, gv_out,
    kx, vx, qb, cb, o_st, gq_st, gk_st, gv_st, g_out, g_in, s_buf, gk_acc, gv_acc, bias_ref,
    in_send, in_recv, in_loc, halo_send, halo_recv, g_send, g_recv, out_send, out_recv, out_loc,
):
    s = lax.axis_index("seq")
    z = lax.axis_index("head")
    has_prev = s > 0
    has_next = s < nseq - 1
    scale = 1.0 / math.sqrt(HD)
    log2_scale = scale * math.log2(math.e)

    peers = [lax.rem(z + d, nz) for d in range(1, nz)]
    ins = (k_in, v_in, q_in, c_in)
    outs = (o_out, gq_out, gk_out, gv_out)
    stages = (o_st, gq_st, gk_st, gv_st)

    def in_place(a, h, source):
        if a < 2:
            start = FRAME + source * rows
            return (kx, vx)[a].at[h, pl.ds(pl.multiple_of(start, 32), rows), :]
        return (qb, cb)[a - 2].at[h, pl.ds(pl.multiple_of(source * rows, 32), rows), :]

    def columns(owner, h):
        return pl.ds(pl.multiple_of((owner * heads + h) * HD, HD), HD)

    def in_copy(a, h, peer, source):
        return pltpu.make_async_remote_copy(
            src_ref=ins[a].at[:, columns(peer, h)],
            dst_ref=in_place(a, h, source),
            send_sem=in_send.at[a, h, peer],
            recv_sem=in_recv.at[a, h, source],
            device_id=(s, peer),
            device_id_type=MESH,
        )

    def in_local(a, h):
        return pltpu.make_async_copy(
            ins[a].at[:, columns(z, h)], in_place(a, h, z), in_loc.at[a, h]
        )

    def out_copy(a, h, peer, source):
        return pltpu.make_async_remote_copy(
            src_ref=stages[a].at[h, pl.ds(pl.multiple_of(peer * rows, 32), rows), :],
            dst_ref=outs[a].at[:, columns(source, h)],
            send_sem=out_send.at[a, h, peer],
            recv_sem=out_recv.at[a, h, source],
            device_id=(s, peer),
            device_id_type=MESH,
        )

    def out_local(a, h):
        return pltpu.make_async_copy(
            stages[a].at[h, pl.ds(pl.multiple_of(z * rows, 32), rows), :],
            outs[a].at[:, columns(z, h)],
            out_loc.at[a, h],
        )

    def halo_copy(a, h, side):
        ext = (kx, vx)[a]
        return pltpu.make_async_remote_copy(
            src_ref=ext.at[h, pl.ds(FRAME, FRAME), :],
            dst_ref=ext.at[h, pl.ds(2 * FRAME * side, FRAME), :],
            send_sem=halo_send.at[a, h, side],
            recv_sem=halo_recv.at[a, h, side],
            device_id=(s + 1 - 2 * side, z),
            device_id_type=MESH,
        )

    def grad_copy(a, h, side):
        return pltpu.make_async_remote_copy(
            src_ref=g_out.at[a, h, side],
            dst_ref=g_in.at[a, h, side],
            send_sem=g_send.at[a, h, side],
            recv_sem=g_recv.at[a, h, side],
            device_id=(s - 1 + 2 * side, z),
            device_id_type=MESH,
        )

    barrier = pltpu.get_barrier_semaphore()
    for peer in peers:
        pl.semaphore_signal(barrier, inc=1, device_id=(s, peer), device_id_type=MESH)

    @pl.when(has_prev)
    def _():
        pl.semaphore_signal(barrier, inc=1, device_id=(s - 1, z), device_id_type=MESH)

    @pl.when(has_next)
    def _():
        pl.semaphore_signal(barrier, inc=1, device_id=(s + 1, z), device_id_type=MESH)

    pl.semaphore_wait(barrier, nz - 1 + has_prev.astype(jnp.int32) + has_next.astype(jnp.int32))

    def start_in(h):
        for a in range(4):
            for peer in peers:
                in_copy(a, h, peer, z).start()
            in_local(a, h).start()

    start_in(0)

    first_tile = s * TILES_F
    ext_rows = 40
    listed = near_ref[...]
    count = listed.shape[1]
    ext_row = lax.broadcasted_iota(jnp.int32, (ext_rows, count), 0)
    present = jnp.zeros((ext_rows, count), F32)
    for k in range(3 * TILES_F):
        tile = first_tile - TILES_F + k
        match = (listed == tile) & (listed >= 0)
        match = jnp.max(jnp.where(match, 1.0, 0.0).astype(F32), axis=0, keepdims=True)
        present = jnp.where(ext_row == k, match, present)
    present = present.astype(BF16)
    tile_row = lax.broadcasted_iota(jnp.int32, (count, ROW), 0)
    lane_tile = first_tile + lax.broadcasted_iota(jnp.int32, (count, ROW), 1) // TILE
    for r in range(TILE_ROWS):
        spread = jnp.where(tile_row == lane_tile + r * TILE_COLS, 1.0, 0.0).astype(BF16)
        bias = jnp.where(dot(present, spread, NN) > 0.5, 0.0, masked_score).astype(F32)
        for n in range(3 * TILE_ROWS):
            bias_ref[r, n, 0:TILE_COLS, :] = bias[n * TILE_COLS : (n + 1) * TILE_COLS, :]

    @pl.when(jnp.logical_not(has_prev))
    def _():
        kx[:, 0:FRAME, :] = jnp.zeros((heads, FRAME, HD), BF16)
        vx[:, 0:FRAME, :] = jnp.zeros((heads, FRAME, HD), BF16)

    @pl.when(jnp.logical_not(has_next))
    def _():
        kx[:, 2 * FRAME : 3 * FRAME, :] = jnp.zeros((heads, FRAME, HD), BF16)
        vx[:, 2 * FRAME : 3 * FRAME, :] = jnp.zeros((heads, FRAME, HD), BF16)

    def wait_in(h, arrays):
        for a in arrays:
            for peer in peers:
                in_copy(a, h, peer, peer).wait_recv()
            in_local(a, h).wait()

    def forward(h):
        wait_in(h, (0, 1))
        for side, there in ((0, has_next), (1, has_prev)):
            @pl.when(there)
            def _(side=side):
                for a in range(2):
                    halo_copy(a, h, side).start()

        @pl.when(h + 1 < heads)
        def _():
            start_in(h + 1)

    def attend(h, r):
        low, high = max(r - 1, 0), min(r + 1, TILE_ROWS - 1)
        near = range(low, high + 1)
        base = r * ROW
        q = qb[h, base : base + ROW, :]
        c = cb[h, base : base + ROW, :]

        def first(f, top):
            for n in near:
                start = pl.multiple_of(f * FRAME + n * ROW, ROW)
                t = dot(kx[h, pl.ds(start, ROW), :], q, NT) * log2_scale
                rows_bias = bias_ref[r, f * TILE_ROWS + n]
                parts = []
                for k in range(TILE_COLS):
                    part = t[k * TILE : (k + 1) * TILE, :] + rows_bias[k : k + 1, :]
                    s_buf[pl.ds(start + k * TILE, TILE), :] = part
                    top = jnp.maximum(top, jnp.max(part.reshape(TILE // 8, 8, ROW), axis=0))
            return top

        top = lax.fori_loop(0, 3, first, jnp.full((8, ROW), masked_score, F32))
        top = jnp.max(top, axis=0, keepdims=True)

        def second(f, carry):
            total, out_t = carry
            for n in near:
                start = pl.multiple_of(f * FRAME + n * ROW, ROW)
                e = jnp.exp2(s_buf[pl.ds(start, ROW), :] - top)
                s_buf[pl.ds(start, ROW), :] = e
                total = total + jnp.sum(e.reshape(ROW // 8, 8, ROW), axis=0)
                out_t = out_t + dot(vx[h, pl.ds(start, ROW), :], e.astype(BF16), TN)
            return total, out_t

        total, out_t = lax.fori_loop(
            0, 3, second, (jnp.zeros((8, ROW), F32), jnp.zeros((HD, ROW), F32))
        )
        inverse = 1.0 / jnp.sum(total, axis=0, keepdims=True)
        out = jnp.transpose(out_t * inverse).astype(BF16)
        o_st[h, base : base + ROW, :] = out
        products = jnp.transpose(out.astype(F32) * c.astype(F32))
        grad_dot = jnp.sum(products, axis=0, keepdims=True)
        inverse_scaled = inverse * scale

        def third(f, gq_t):
            for n in near:
                start = pl.multiple_of(f * FRAME + n * ROW, ROW)
                here = pl.ds(start, ROW)
                e = s_buf[here, :]
                gp = dot(vx[h, here, :], c, NT)
                p_low = (e * inverse).astype(BF16)
                gs = ((e * inverse_scaled) * (gp - grad_dot)).astype(BF16)
                gv = dot(p_low, c, NN)
                gk = dot(gs, q, NN)
                if r == max(n - 1, 0):
                    gv_acc[here, :] = gv
                    gk_acc[here, :] = gk
                else:
                    gv_acc[here, :] += gv
                    gk_acc[here, :] += gk
                gq_t = gq_t + dot(kx[h, here, :], gs, TN)
            return gq_t

        gq_t = lax.fori_loop(0, 3, third, jnp.zeros((HD, ROW), F32))
        gq_st[h, base : base + ROW, :] = jnp.transpose(gq_t).astype(BF16)

    def send_out(a, h):
        for peer in peers:
            out_copy(a, h, peer, z).start()
        out_local(a, h).start()

    def finish(h):
        for side, there in ((1, has_prev), (0, has_next)):
            @pl.when(there)
            def _(side=side):
                for a in range(2):
                    grad_copy(a, h, side).wait_recv()
                    acc = (gk_acc, gv_acc)[a]
                    acc[FRAME : 2 * FRAME, :] += g_in[a, h, side].astype(F32)
        for a in range(2):
            stages[2 + a][h] = (gk_acc, gv_acc)[a][FRAME : 2 * FRAME, :].astype(BF16)

    forward(0)

    def one_head(h, _):
        wait_in(h, (2, 3))
        for side, there in ((0, has_prev), (1, has_next)):
            @pl.when(there)
            def _(side=side):
                for a in range(2):
                    halo_copy(a, h, side).wait_recv()

        @pl.when(h > 0)
        def _():
            finish(h - 1)
            send_out(2, h - 1)
            send_out(3, h - 1)

        for r in range(TILE_ROWS):
            attend(h, r)
        for side, there in ((0, has_prev), (1, has_next)):
            @pl.when(there)
            def _(side=side):
                for a in range(2):
                    part = (gk_acc, gv_acc)[a][pl.ds(2 * FRAME * side, FRAME), :]
                    g_out[a, h, side] = part.astype(BF16)
                    grad_copy(a, h, side).start()

        @pl.when(h + 1 < heads)
        def _():
            forward(h + 1)

        send_out(0, h)
        send_out(1, h)
        return 0

    lax.fori_loop(0, heads, one_head, 0)
    finish(heads - 1)
    send_out(2, heads - 1)
    send_out(3, heads - 1)

    def drain(h, _):
        for a in range(4):
            for peer in peers:
                in_copy(a, h, peer, z).wait_send()
                out_copy(a, h, peer, z).wait_send()
                out_copy(a, h, peer, peer).wait_recv()
            out_local(a, h).wait()
        for a in range(2):
            for side, there, back in ((0, has_next, has_prev), (1, has_prev, has_next)):
                @pl.when(there)
                def _(a=a, side=side):
                    halo_copy(a, h, side).wait_send()

                @pl.when(back)
                def _(a=a, side=side):
                    grad_copy(a, h, side).wait_send()
        return 0

    lax.fori_loop(0, heads, drain, 0)


def place_results(*refs):
    for a in range(4):
        refs[4 + a][...] = refs[a][...]


def shards(nseq, nz, queries, keys, values, cotangent, neighbours):
    rows, width = queries.shape
    heads = width // HD // nz
    vmem = pl.BlockSpec(memory_space=pltpu.VMEM)
    dma = pltpu.SemaphoreType.DMA
    results = pl.pallas_call(
        functools.partial(kernel, nseq, nz, heads, rows),
        out_shape=[jax.ShapeDtypeStruct((rows, width), BF16)] * 4,
        in_specs=[vmem] * 5,
        out_specs=[vmem] * 4,
        scratch_shapes=[
            pltpu.VMEM((heads, 3 * FRAME, HD), BF16),
            pltpu.VMEM((heads, 3 * FRAME, HD), BF16),
            pltpu.VMEM((heads, FRAME, HD), BF16),
            pltpu.VMEM((heads, FRAME, HD), BF16),
            pltpu.VMEM((heads, FRAME, HD), BF16),
            pltpu.VMEM((heads, FRAME, HD), BF16),
            pltpu.VMEM((heads, FRAME, HD), BF16),
            pltpu.VMEM((heads, FRAME, HD), BF16),
            pltpu.VMEM((2, heads, 2, FRAME, HD), BF16),
            pltpu.VMEM((2, heads, 2, FRAME, HD), BF16),
            pltpu.VMEM((3 * FRAME, ROW), F32),
            pltpu.VMEM((3 * FRAME, HD), F32),
            pltpu.VMEM((3 * FRAME, HD), F32),
            pltpu.VMEM((TILE_ROWS, 3 * TILE_ROWS, 8, ROW), F32),
            dma((4, heads, nz)),
            dma((4, heads, nz)),
            dma((4, heads)),
            dma((2, heads, 2)),
            dma((2, heads, 2)),
            dma((2, heads, 2)),
            dma((2, heads, 2)),
            dma((4, heads, nz)),
            dma((4, heads, nz)),
            dma((4, heads)),
        ],
        compiler_params=pltpu.CompilerParams(
            collective_id=0, has_side_effects=True, vmem_limit_bytes=56 * 1024 * 1024
        ),
    )(keys, values, queries, cotangent, neighbours.T)
    block_rows = 48 if rows % 48 == 0 else rows
    block = pl.BlockSpec((block_rows, width), lambda i: (i, 0))
    return pl.pallas_call(
        place_results,
        grid=(rows // block_rows,),
        out_shape=[jax.ShapeDtypeStruct((rows, width), BF16)] * 4,
        in_specs=[block] * 4,
        out_specs=[block] * 4,
        compiler_params=pltpu.CompilerParams(vmem_limit_bytes=56 * 1024 * 1024),
    )(*results)


def solution(mesh):
    placed = P(("seq", "head"), None)
    return jax.shard_map(
        functools.partial(shards, mesh.shape["seq"], mesh.shape["head"]),
        mesh=mesh,
        in_specs=(placed, placed, placed, placed, P()),
        out_specs=(placed, placed, placed, placed),
        check_vma=False,
    )
```

```python
import functools
import math

import jax
import jax.numpy as jnp
from jax import lax
from jax.experimental import pallas as pl
from jax.experimental.pallas import tpu as pltpu
from jax.sharding import PartitionSpec as P

TILE = 64
TILE_ROWS = 3
TILE_COLS = 4
TILES_F = 12
HD = 128
FRAME = TILE * TILES_F
ROW = TILE * TILE_COLS
MESH = pl.DeviceIdType.MESH
masked_score = -1e30
F32 = jnp.float32
BF16 = jnp.bfloat16

NT = (((1,), (1,)), ((), ()))
TN = (((0,), (0,)), ((), ()))
NN = (((1,), (0,)), ((), ()))


def dot(a, b, dims):
    return lax.dot_general(a, b, dims, preferred_element_type=F32)


def kernel(
    nseq, nz, heads, rows,
    k_in, v_in, q_in, c_in, near_ref,
    o_out, gq_out, gk_out, gv_out,
    kx, vx, qb, cb, o_st, gq_st, gk_st, gv_st, g_out, g_in, s_buf, gk_acc, gv_acc, bias_ref, own,
    in_send, in_recv, in_loc, halo_send, halo_recv, g_send, g_recv, out_send, out_recv, out_loc,
):
    s = lax.axis_index("seq")
    z = lax.axis_index("head")
    has_prev = s > 0
    has_next = s < nseq - 1
    scale = 1.0 / math.sqrt(HD)
    log2_scale = scale * math.log2(math.e)

    peers = [lax.rem(z + d, nz) for d in range(1, nz)]
    ins = (k_in, v_in, q_in, c_in)
    outs = (o_out, gq_out, gk_out, gv_out)
    stages = (o_st, gq_st, gk_st, gv_st)

    def in_place(a, h, source):
        if a < 2:
            start = FRAME + source * rows
            return (kx, vx)[a].at[h, pl.ds(pl.multiple_of(start, 32), rows), :]
        return (qb, cb)[a - 2].at[h, pl.ds(pl.multiple_of(source * rows, 32), rows), :]

    def columns(owner, h):
        return pl.ds(pl.multiple_of((owner * heads + h) * HD, HD), HD)

    def in_copy(a, h, peer, source):
        return pltpu.make_async_remote_copy(
            src_ref=ins[a].at[:, columns(peer, h)],
            dst_ref=in_place(a, h, source),
            send_sem=in_send.at[a, h, peer],
            recv_sem=in_recv.at[a, h, source],
            device_id=(s, peer),
            device_id_type=MESH,
        )

    def in_local(a, h):
        return pltpu.make_async_copy(
            ins[a].at[:, columns(z, h)], in_place(a, h, z), in_loc.at[a, h]
        )

    def out_copy(a, h, peer, source):
        return pltpu.make_async_remote_copy(
            src_ref=stages[a].at[h, pl.ds(pl.multiple_of(peer * rows, 32), rows), :],
            dst_ref=outs[a].at[:, columns(source, h)],
            send_sem=out_send.at[a, h, peer],
            recv_sem=out_recv.at[a, h, source],
            device_id=(s, peer),
            device_id_type=MESH,
        )

    def out_local(a, h):
        return pltpu.make_async_copy(
            stages[a].at[h, pl.ds(pl.multiple_of(z * rows, 32), rows), :],
            outs[a].at[:, columns(z, h)],
            out_loc.at[a, h],
        )

    def halo_copy(a, h, side):
        ext = (kx, vx)[a]
        return pltpu.make_async_remote_copy(
            src_ref=ext.at[h, pl.ds(FRAME, FRAME), :],
            dst_ref=ext.at[h, pl.ds(2 * FRAME * side, FRAME), :],
            send_sem=halo_send.at[a, h, side],
            recv_sem=halo_recv.at[a, h, side],
            device_id=(s + 1 - 2 * side, z),
            device_id_type=MESH,
        )

    def grad_copy(a, h, side):
        return pltpu.make_async_remote_copy(
            src_ref=g_out.at[a, h, side],
            dst_ref=g_in.at[a, h, side],
            send_sem=g_send.at[a, h, side],
            recv_sem=g_recv.at[a, h, side],
            device_id=(s - 1 + 2 * side, z),
            device_id_type=MESH,
        )

    barrier = pltpu.get_barrier_semaphore()
    for peer in peers:
        pl.semaphore_signal(barrier, inc=1, device_id=(s, peer), device_id_type=MESH)

    @pl.when(has_prev)
    def _():
        pl.semaphore_signal(barrier, inc=1, device_id=(s - 1, z), device_id_type=MESH)

    @pl.when(has_next)
    def _():
        pl.semaphore_signal(barrier, inc=1, device_id=(s + 1, z), device_id_type=MESH)

    pl.semaphore_wait(barrier, nz - 1 + has_prev.astype(jnp.int32) + has_next.astype(jnp.int32))

    def start_in(h):
        for a in range(4):
            for peer in peers:
                in_copy(a, h, peer, z).start()
            in_local(a, h).start()

    start_in(0)

    first_tile = s * TILES_F
    ext_rows = 40
    listed = near_ref[...]
    count = listed.shape[1]
    ext_row = lax.broadcasted_iota(jnp.int32, (ext_rows, count), 0)
    present = jnp.zeros((ext_rows, count), F32)
    for k in range(3 * TILES_F):
        tile = first_tile - TILES_F + k
        match = (listed == tile) & (listed >= 0)
        match = jnp.max(jnp.where(match, 1.0, 0.0).astype(F32), axis=0, keepdims=True)
        present = jnp.where(ext_row == k, match, present)
    present = present.astype(BF16)
    tile_row = lax.broadcasted_iota(jnp.int32, (count, ROW), 0)
    lane_tile = first_tile + lax.broadcasted_iota(jnp.int32, (count, ROW), 1) // TILE
    for r in range(TILE_ROWS):
        spread = jnp.where(tile_row == lane_tile + r * TILE_COLS, 1.0, 0.0).astype(BF16)
        bias = jnp.where(dot(present, spread, NN) > 0.5, 0.0, masked_score).astype(F32)
        for n in range(3 * TILE_ROWS):
            bias_ref[r, n, 0:TILE_COLS, :] = bias[n * TILE_COLS : (n + 1) * TILE_COLS, :]

    @pl.when(jnp.logical_not(has_prev))
    def _():
        kx[:, 0:FRAME, :] = jnp.zeros((heads, FRAME, HD), BF16)
        vx[:, 0:FRAME, :] = jnp.zeros((heads, FRAME, HD), BF16)

    @pl.when(jnp.logical_not(has_next))
    def _():
        kx[:, 2 * FRAME : 3 * FRAME, :] = jnp.zeros((heads, FRAME, HD), BF16)
        vx[:, 2 * FRAME : 3 * FRAME, :] = jnp.zeros((heads, FRAME, HD), BF16)

    def wait_in(h, arrays):
        for a in arrays:
            for peer in peers:
                in_copy(a, h, peer, peer).wait_recv()
            in_local(a, h).wait()

    def forward(h):
        wait_in(h, (0, 1))
        for side, there in ((0, has_next), (1, has_prev)):
            @pl.when(there)
            def _(side=side):
                for a in range(2):
                    halo_copy(a, h, side).start()

        @pl.when(h + 1 < heads)
        def _():
            start_in(h + 1)

    def attend(h, r):
        low, high = max(r - 1, 0), min(r + 1, TILE_ROWS - 1)
        near = range(low, high + 1)
        base = r * ROW
        q = qb[h, base : base + ROW, :]
        c = cb[h, base : base + ROW, :]

        def first(f, top):
            for n in near:
                start = pl.multiple_of(f * FRAME + n * ROW, ROW)
                t = dot(kx[h, pl.ds(start, ROW), :], q, NT) * log2_scale
                rows_bias = bias_ref[r, f * TILE_ROWS + n]
                parts = []
                for k in range(TILE_COLS):
                    part = t[k * TILE : (k + 1) * TILE, :] + rows_bias[k : k + 1, :]
                    s_buf[pl.ds(start + k * TILE, TILE), :] = part
                    top = jnp.maximum(top, jnp.max(part.reshape(TILE // 8, 8, ROW), axis=0))
            return top

        top = lax.fori_loop(0, 3, first, jnp.full((8, ROW), masked_score, F32))
        top = jnp.max(top, axis=0, keepdims=True)

        def second(f, carry):
            total, out_t = carry
            for n in near:
                start = pl.multiple_of(f * FRAME + n * ROW, ROW)
                e = jnp.exp2(s_buf[pl.ds(start, ROW), :] - top)
                s_buf[pl.ds(start, ROW), :] = e
                total = total + jnp.sum(e.reshape(ROW // 8, 8, ROW), axis=0)
                out_t = out_t + dot(vx[h, pl.ds(start, ROW), :], e.astype(BF16), TN)
            return total, out_t

        total, out_t = lax.fori_loop(
            0, 3, second, (jnp.zeros((8, ROW), F32), jnp.zeros((HD, ROW), F32))
        )
        inverse = 1.0 / jnp.sum(total, axis=0, keepdims=True)
        out = jnp.transpose(out_t * inverse).astype(BF16)
        o_st[h, base : base + ROW, :] = out
        products = jnp.transpose(out.astype(F32) * c.astype(F32))
        grad_dot = jnp.sum(products, axis=0, keepdims=True)
        inverse_scaled = inverse * scale

        def third(f, gq_t):
            for n in near:
                start = pl.multiple_of(f * FRAME + n * ROW, ROW)
                here = pl.ds(start, ROW)
                e = s_buf[here, :]
                gp = dot(vx[h, here, :], c, NT)
                p_low = (e * inverse).astype(BF16)
                gs = ((e * inverse_scaled) * (gp - grad_dot)).astype(BF16)
                gv = dot(p_low, c, NN)
                gk = dot(gs, q, NN)
                if r == max(n - 1, 0):
                    gv_acc[here, :] = gv
                    gk_acc[here, :] = gk
                else:
                    gv_acc[here, :] += gv
                    gk_acc[here, :] += gk
                gq_t = gq_t + dot(kx[h, here, :], gs, TN)
            return gq_t

        gq_t = lax.fori_loop(0, 3, third, jnp.zeros((HD, ROW), F32))
        gq_st[h, base : base + ROW, :] = jnp.transpose(gq_t).astype(BF16)

    def send_out(a, h):
        for peer in peers:
            out_copy(a, h, peer, z).start()
        out_local(a, h).start()

    def finish(h):
        for side, there in ((1, has_prev), (0, has_next)):
            @pl.when(there)
            def _(side=side):
                for a in range(2):
                    grad_copy(a, h, side).wait_recv()
                    own[a] += g_in[a, h, side].astype(F32)
        for a in range(2):
            stages[2 + a][h] = own[a].astype(BF16)

    forward(0)

    def one_head(h, _):
        wait_in(h, (2, 3))
        for side, there in ((0, has_prev), (1, has_next)):
            @pl.when(there)
            def _(side=side):
                for a in range(2):
                    halo_copy(a, h, side).wait_recv()

        attend(h, 0)
        attend(h, 1)

        @pl.when(h + 1 < heads)
        def _():
            forward(h + 1)

        @pl.when(h > 0)
        def _():
            finish(h - 1)
            send_out(2, h - 1)
            send_out(3, h - 1)

        attend(h, 2)
        for a in range(2):
            own[a] = (gk_acc, gv_acc)[a][FRAME : 2 * FRAME, :]
        for side, there in ((0, has_prev), (1, has_next)):
            @pl.when(there)
            def _(side=side):
                for a in range(2):
                    part = (gk_acc, gv_acc)[a][pl.ds(2 * FRAME * side, FRAME), :]
                    g_out[a, h, side] = part.astype(BF16)
                    grad_copy(a, h, side).start()

        send_out(0, h)
        send_out(1, h)
        return 0

    lax.fori_loop(0, heads, one_head, 0)
    finish(heads - 1)
    send_out(2, heads - 1)
    send_out(3, heads - 1)

    def drain(h, _):
        for a in range(4):
            for peer in peers:
                in_copy(a, h, peer, z).wait_send()
                out_copy(a, h, peer, z).wait_send()
                out_copy(a, h, peer, peer).wait_recv()
            out_local(a, h).wait()
        for a in range(2):
            for side, there, back in ((0, has_next, has_prev), (1, has_prev, has_next)):
                @pl.when(there)
                def _(a=a, side=side):
                    halo_copy(a, h, side).wait_send()

                @pl.when(back)
                def _(a=a, side=side):
                    grad_copy(a, h, side).wait_send()
        return 0

    lax.fori_loop(0, heads, drain, 0)


def place_results(*refs):
    for a in range(4):
        refs[4 + a][...] = refs[a][...]


def shards(nseq, nz, queries, keys, values, cotangent, neighbours):
    rows, width = queries.shape
    heads = width // HD // nz
    place = pl.BlockSpec(memory_space=pl.ANY)
    dma = pltpu.SemaphoreType.DMA
    results = pl.pallas_call(
        functools.partial(kernel, nseq, nz, heads, rows),
        out_shape=[jax.ShapeDtypeStruct((rows, width), BF16)] * 4,
        in_specs=[place] * 4 + [pl.BlockSpec(memory_space=pltpu.VMEM)],
        out_specs=[place] * 4,
        scratch_shapes=[
            pltpu.VMEM((heads, 3 * FRAME, HD), BF16),
            pltpu.VMEM((heads, 3 * FRAME, HD), BF16),
            pltpu.VMEM((heads, FRAME, HD), BF16),
            pltpu.VMEM((heads, FRAME, HD), BF16),
            pltpu.VMEM((heads, FRAME, HD), BF16),
            pltpu.VMEM((heads, FRAME, HD), BF16),
            pltpu.VMEM((heads, FRAME, HD), BF16),
            pltpu.VMEM((heads, FRAME, HD), BF16),
            pltpu.VMEM((2, heads, 2, FRAME, HD), BF16),
            pltpu.VMEM((2, heads, 2, FRAME, HD), BF16),
            pltpu.VMEM((3 * FRAME, ROW), F32),
            pltpu.VMEM((3 * FRAME, HD), F32),
            pltpu.VMEM((3 * FRAME, HD), F32),
            pltpu.VMEM((TILE_ROWS, 3 * TILE_ROWS, 8, ROW), F32),
            pltpu.VMEM((2, FRAME, HD), F32),
            dma((4, heads, nz)),
            dma((4, heads, nz)),
            dma((4, heads)),
            dma((2, heads, 2)),
            dma((2, heads, 2)),
            dma((2, heads, 2)),
            dma((2, heads, 2)),
            dma((4, heads, nz)),
            dma((4, heads, nz)),
            dma((4, heads)),
        ],
        compiler_params=pltpu.CompilerParams(
            collective_id=0, has_side_effects=True, vmem_limit_bytes=56 * 1024 * 1024
        ),
    )(keys, values, queries, cotangent, neighbours.T)
    block_rows = 48 if rows % 48 == 0 else rows
    block = pl.BlockSpec((block_rows, width), lambda i: (i, 0))
    return pl.pallas_call(
        place_results,
        grid=(rows // block_rows,),
        out_shape=[jax.ShapeDtypeStruct((rows, width), BF16)] * 4,
        in_specs=[block] * 4,
        out_specs=[block] * 4,
        compiler_params=pltpu.CompilerParams(vmem_limit_bytes=56 * 1024 * 1024),
    )(*results)


def solution(mesh):
    placed = P(("seq", "head"), None)
    return jax.shard_map(
        functools.partial(shards, mesh.shape["seq"], mesh.shape["head"]),
        mesh=mesh,
        in_specs=(placed, placed, placed, placed, P()),
        out_specs=(placed, placed, placed, placed),
        check_vma=False,
    )
```

```python
import functools
import math

import jax
import jax.numpy as jnp
from jax import lax
from jax.experimental import pallas as pl
from jax.experimental.pallas import tpu as pltpu
from jax.sharding import PartitionSpec as P

TILE = 64
TILE_ROWS = 3
TILE_COLS = 4
TILES_F = 12
HD = 128
FRAME = TILE * TILES_F
ROW = TILE * TILE_COLS
MESH = pl.DeviceIdType.MESH
masked_score = -1e30
F32 = jnp.float32
BF16 = jnp.bfloat16

NT = (((1,), (1,)), ((), ()))
TN = (((0,), (0,)), ((), ()))
NN = (((1,), (0,)), ((), ()))


def dot(a, b, dims):
    return lax.dot_general(a, b, dims, preferred_element_type=F32)


def kernel(
    nseq, nz, heads, rows,
    k_in, v_in, q_in, c_in, near_ref,
    o_out, gq_out, gk_out, gv_out,
    kx, vx, qb, cb, o_st, gq_st, gk_st, gv_st, g_out, g_in, s_buf, gk_acc, gv_acc, bias_ref, own,
    in_send, in_recv, in_loc, halo_send, halo_recv, g_send, g_recv, out_send, out_recv, out_loc,
):
    s = lax.axis_index("seq")
    z = lax.axis_index("head")
    has_prev = s > 0
    has_next = s < nseq - 1
    scale = 1.0 / math.sqrt(HD)
    log2_scale = scale * math.log2(math.e)

    peers = [lax.rem(z + d, nz) for d in range(1, nz)]
    ins = (k_in, v_in, q_in, c_in)
    outs = (o_out, gq_out, gk_out, gv_out)
    stages = (o_st, gq_st, gk_st, gv_st)

    def in_place(a, h, source):
        if a < 2:
            start = FRAME + source * rows
            return (kx, vx)[a].at[h, pl.ds(pl.multiple_of(start, 32), rows), :]
        return (qb, cb)[a - 2].at[h, pl.ds(pl.multiple_of(source * rows, 32), rows), :]

    def columns(owner, h):
        return pl.ds(pl.multiple_of((owner * heads + h) * HD, HD), HD)

    def in_copy(a, h, peer, source):
        return pltpu.make_async_remote_copy(
            src_ref=ins[a].at[:, columns(peer, h)],
            dst_ref=in_place(a, h, source),
            send_sem=in_send.at[a, h, peer],
            recv_sem=in_recv.at[a, h, source],
            device_id=(s, peer),
            device_id_type=MESH,
        )

    def in_local(a, h):
        return pltpu.make_async_copy(
            ins[a].at[:, columns(z, h)], in_place(a, h, z), in_loc.at[a, h]
        )

    def out_copy(a, h, peer, source):
        return pltpu.make_async_remote_copy(
            src_ref=stages[a].at[h, pl.ds(pl.multiple_of(peer * rows, 32), rows), :],
            dst_ref=outs[a].at[source * heads + h],
            send_sem=out_send.at[a, h, peer],
            recv_sem=out_recv.at[a, h, source],
            device_id=(s, peer),
            device_id_type=MESH,
        )

    def out_local(a, h):
        return pltpu.make_async_copy(
            stages[a].at[h, pl.ds(pl.multiple_of(z * rows, 32), rows), :],
            outs[a].at[z * heads + h],
            out_loc.at[a, h],
        )

    def halo_copy(a, h, side):
        ext = (kx, vx)[a]
        return pltpu.make_async_remote_copy(
            src_ref=ext.at[h, pl.ds(FRAME, FRAME), :],
            dst_ref=ext.at[h, pl.ds(2 * FRAME * side, FRAME), :],
            send_sem=halo_send.at[a, h, side],
            recv_sem=halo_recv.at[a, h, side],
            device_id=(s + 1 - 2 * side, z),
            device_id_type=MESH,
        )

    def grad_copy(a, h, side):
        return pltpu.make_async_remote_copy(
            src_ref=g_out.at[a, h, side],
            dst_ref=g_in.at[a, h, side],
            send_sem=g_send.at[a, h, side],
            recv_sem=g_recv.at[a, h, side],
            device_id=(s - 1 + 2 * side, z),
            device_id_type=MESH,
        )

    barrier = pltpu.get_barrier_semaphore()
    for peer in peers:
        pl.semaphore_signal(barrier, inc=1, device_id=(s, peer), device_id_type=MESH)

    @pl.when(has_prev)
    def _():
        pl.semaphore_signal(barrier, inc=1, device_id=(s - 1, z), device_id_type=MESH)

    @pl.when(has_next)
    def _():
        pl.semaphore_signal(barrier, inc=1, device_id=(s + 1, z), device_id_type=MESH)

    pl.semaphore_wait(barrier, nz - 1 + has_prev.astype(jnp.int32) + has_next.astype(jnp.int32))

    def start_in(h):
        for a in range(4):
            for peer in peers:
                in_copy(a, h, peer, z).start()
            in_local(a, h).start()

    start_in(0)

    first_tile = s * TILES_F
    ext_rows = 40
    listed = near_ref[...]
    count = listed.shape[1]
    ext_row = lax.broadcasted_iota(jnp.int32, (ext_rows, count), 0)
    present = jnp.zeros((ext_rows, count), F32)
    for k in range(3 * TILES_F):
        tile = first_tile - TILES_F + k
        match = (listed == tile) & (listed >= 0)
        match = jnp.max(jnp.where(match, 1.0, 0.0).astype(F32), axis=0, keepdims=True)
        present = jnp.where(ext_row == k, match, present)
    present = present.astype(BF16)
    tile_row = lax.broadcasted_iota(jnp.int32, (count, ROW), 0)
    lane_tile = first_tile + lax.broadcasted_iota(jnp.int32, (count, ROW), 1) // TILE
    for r in range(TILE_ROWS):
        spread = jnp.where(tile_row == lane_tile + r * TILE_COLS, 1.0, 0.0).astype(BF16)
        bias = jnp.where(dot(present, spread, NN) > 0.5, 0.0, masked_score).astype(F32)
        for n in range(3 * TILE_ROWS):
            bias_ref[r, n, 0:TILE_COLS, :] = bias[n * TILE_COLS : (n + 1) * TILE_COLS, :]

    @pl.when(jnp.logical_not(has_prev))
    def _():
        kx[:, 0:FRAME, :] = jnp.zeros((heads, FRAME, HD), BF16)
        vx[:, 0:FRAME, :] = jnp.zeros((heads, FRAME, HD), BF16)

    @pl.when(jnp.logical_not(has_next))
    def _():
        kx[:, 2 * FRAME : 3 * FRAME, :] = jnp.zeros((heads, FRAME, HD), BF16)
        vx[:, 2 * FRAME : 3 * FRAME, :] = jnp.zeros((heads, FRAME, HD), BF16)

    def wait_in(h, arrays):
        for a in arrays:
            for peer in peers:
                in_copy(a, h, peer, peer).wait_recv()
            in_local(a, h).wait()

    def forward(h):
        wait_in(h, (0, 1))
        for side, there in ((0, has_next), (1, has_prev)):
            @pl.when(there)
            def _(side=side):
                for a in range(2):
                    halo_copy(a, h, side).start()

        @pl.when(h + 1 < heads)
        def _():
            start_in(h + 1)

    def attend(h, r):
        low, high = max(r - 1, 0), min(r + 1, TILE_ROWS - 1)
        near = range(low, high + 1)
        base = r * ROW
        q = qb[h, base : base + ROW, :]
        c = cb[h, base : base + ROW, :]

        def first(f, top):
            for n in near:
                start = pl.multiple_of(f * FRAME + n * ROW, ROW)
                t = dot(kx[h, pl.ds(start, ROW), :], q, NT) * log2_scale
                rows_bias = bias_ref[r, f * TILE_ROWS + n]
                parts = []
                for k in range(TILE_COLS):
                    part = t[k * TILE : (k + 1) * TILE, :] + rows_bias[k : k + 1, :]
                    s_buf[pl.ds(start + k * TILE, TILE), :] = part
                    top = jnp.maximum(top, jnp.max(part.reshape(TILE // 8, 8, ROW), axis=0))
            return top

        top = lax.fori_loop(0, 3, first, jnp.full((8, ROW), masked_score, F32))
        top = jnp.max(top, axis=0, keepdims=True)

        def second(f, carry):
            total, out_t = carry
            for n in near:
                start = pl.multiple_of(f * FRAME + n * ROW, ROW)
                e = jnp.exp2(s_buf[pl.ds(start, ROW), :] - top)
                s_buf[pl.ds(start, ROW), :] = e
                total = total + jnp.sum(e.reshape(ROW // 8, 8, ROW), axis=0)
                out_t = out_t + dot(vx[h, pl.ds(start, ROW), :], e.astype(BF16), TN)
            return total, out_t

        total, out_t = lax.fori_loop(
            0, 3, second, (jnp.zeros((8, ROW), F32), jnp.zeros((HD, ROW), F32))
        )
        inverse = 1.0 / jnp.sum(total, axis=0, keepdims=True)
        out = jnp.transpose(out_t * inverse).astype(BF16)
        o_st[h, base : base + ROW, :] = out
        products = jnp.transpose(out.astype(F32) * c.astype(F32))
        grad_dot = jnp.sum(products, axis=0, keepdims=True)
        inverse_scaled = inverse * scale

        def third(f, gq_t):
            for n in near:
                start = pl.multiple_of(f * FRAME + n * ROW, ROW)
                here = pl.ds(start, ROW)
                e = s_buf[here, :]
                gp = dot(vx[h, here, :], c, NT)
                p_low = (e * inverse).astype(BF16)
                gs = ((e * inverse_scaled) * (gp - grad_dot)).astype(BF16)
                gv = dot(p_low, c, NN)
                gk = dot(gs, q, NN)
                if r == max(n - 1, 0):
                    gv_acc[here, :] = gv
                    gk_acc[here, :] = gk
                else:
                    gv_acc[here, :] += gv
                    gk_acc[here, :] += gk
                gq_t = gq_t + dot(kx[h, here, :], gs, TN)
            return gq_t

        gq_t = lax.fori_loop(0, 3, third, jnp.zeros((HD, ROW), F32))
        gq_st[h, base : base + ROW, :] = jnp.transpose(gq_t).astype(BF16)

    def send_out(a, h):
        for peer in peers:
            out_copy(a, h, peer, z).start()
        out_local(a, h).start()

    def finish(h):
        for side, there in ((1, has_prev), (0, has_next)):
            @pl.when(there)
            def _(side=side):
                for a in range(2):
                    grad_copy(a, h, side).wait_recv()
                    own[a] += g_in[a, h, side].astype(F32)
        for a in range(2):
            stages[2 + a][h] = own[a].astype(BF16)

    forward(0)

    def one_head(h, _):
        wait_in(h, (2, 3))
        for side, there in ((0, has_prev), (1, has_next)):
            @pl.when(there)
            def _(side=side):
                for a in range(2):
                    halo_copy(a, h, side).wait_recv()

        attend(h, 0)
        attend(h, 1)

        @pl.when(h + 1 < heads)
        def _():
            forward(h + 1)

        @pl.when(h > 0)
        def _():
            finish(h - 1)
            send_out(2, h - 1)
            send_out(3, h - 1)

        attend(h, 2)
        for a in range(2):
            own[a] = (gk_acc, gv_acc)[a][FRAME : 2 * FRAME, :]
        for side, there in ((0, has_prev), (1, has_next)):
            @pl.when(there)
            def _(side=side):
                for a in range(2):
                    part = (gk_acc, gv_acc)[a][pl.ds(2 * FRAME * side, FRAME), :]
                    g_out[a, h, side] = part.astype(BF16)
                    grad_copy(a, h, side).start()

        send_out(0, h)
        send_out(1, h)
        return 0

    lax.fori_loop(0, heads, one_head, 0)
    finish(heads - 1)
    send_out(2, heads - 1)
    send_out(3, heads - 1)

    def drain(h, _):
        for a in range(4):
            for peer in peers:
                in_copy(a, h, peer, z).wait_send()
                out_copy(a, h, peer, z).wait_send()
                out_copy(a, h, peer, peer).wait_recv()
            out_local(a, h).wait()
        for a in range(2):
            for side, there, back in ((0, has_next, has_prev), (1, has_prev, has_next)):
                @pl.when(there)
                def _(a=a, side=side):
                    halo_copy(a, h, side).wait_send()

                @pl.when(back)
                def _(a=a, side=side):
                    grad_copy(a, h, side).wait_send()
        return 0

    lax.fori_loop(0, heads, drain, 0)


def place_results(*refs):
    for a in range(4):
        for g in range(refs[a].shape[0]):
            refs[4 + a][:, g * HD : (g + 1) * HD] = refs[a][g]


def shards(nseq, nz, queries, keys, values, cotangent, neighbours):
    rows, width = queries.shape
    heads = width // HD // nz
    place = pl.BlockSpec(memory_space=pl.ANY)
    dma = pltpu.SemaphoreType.DMA
    results = pl.pallas_call(
        functools.partial(kernel, nseq, nz, heads, rows),
        out_shape=[jax.ShapeDtypeStruct((width // HD, rows, HD), BF16)] * 4,
        in_specs=[place] * 4 + [pl.BlockSpec(memory_space=pltpu.VMEM)],
        out_specs=[place] * 4,
        scratch_shapes=[
            pltpu.VMEM((heads, 3 * FRAME, HD), BF16),
            pltpu.VMEM((heads, 3 * FRAME, HD), BF16),
            pltpu.VMEM((heads, FRAME, HD), BF16),
            pltpu.VMEM((heads, FRAME, HD), BF16),
            pltpu.VMEM((heads, FRAME, HD), BF16),
            pltpu.VMEM((heads, FRAME, HD), BF16),
            pltpu.VMEM((heads, FRAME, HD), BF16),
            pltpu.VMEM((heads, FRAME, HD), BF16),
            pltpu.VMEM((2, heads, 2, FRAME, HD), BF16),
            pltpu.VMEM((2, heads, 2, FRAME, HD), BF16),
            pltpu.VMEM((3 * FRAME, ROW), F32),
            pltpu.VMEM((3 * FRAME, HD), F32),
            pltpu.VMEM((3 * FRAME, HD), F32),
            pltpu.VMEM((TILE_ROWS, 3 * TILE_ROWS, 8, ROW), F32),
            pltpu.VMEM((2, FRAME, HD), F32),
            dma((4, heads, nz)),
            dma((4, heads, nz)),
            dma((4, heads)),
            dma((2, heads, 2)),
            dma((2, heads, 2)),
            dma((2, heads, 2)),
            dma((2, heads, 2)),
            dma((4, heads, nz)),
            dma((4, heads, nz)),
            dma((4, heads)),
        ],
        compiler_params=pltpu.CompilerParams(
            collective_id=0, has_side_effects=True, vmem_limit_bytes=56 * 1024 * 1024
        ),
    )(keys, values, queries, cotangent, neighbours.T)
    block_rows = 48 if rows % 48 == 0 else rows
    block = pl.BlockSpec((block_rows, width), lambda i: (i, 0))
    by_head = pl.BlockSpec((width // HD, block_rows, HD), lambda i: (0, i, 0))
    return pl.pallas_call(
        place_results,
        grid=(rows // block_rows,),
        out_shape=[jax.ShapeDtypeStruct((rows, width), BF16)] * 4,
        in_specs=[by_head] * 4,
        out_specs=[block] * 4,
        compiler_params=pltpu.CompilerParams(vmem_limit_bytes=56 * 1024 * 1024),
    )(*results)


def solution(mesh):
    placed = P(("seq", "head"), None)
    return jax.shard_map(
        functools.partial(shards, mesh.shape["seq"], mesh.shape["head"]),
        mesh=mesh,
        in_specs=(placed, placed, placed, placed, P()),
        out_specs=(placed, placed, placed, placed),
        check_vma=False,
    )
```

```python
import functools
import math

import jax
import jax.numpy as jnp
from jax import lax
from jax.experimental import pallas as pl
from jax.experimental.pallas import tpu as pltpu
from jax.sharding import PartitionSpec as P

TILE = 64
TILE_ROWS = 3
TILE_COLS = 4
TILES_F = 12
HD = 128
FRAME = TILE * TILES_F
ROW = TILE * TILE_COLS
MESH = pl.DeviceIdType.MESH
masked_score = -1e30
F32 = jnp.float32
BF16 = jnp.bfloat16

NT = (((1,), (1,)), ((), ()))
TN = (((0,), (0,)), ((), ()))
NN = (((1,), (0,)), ((), ()))


def dot(a, b, dims):
    return lax.dot_general(a, b, dims, preferred_element_type=F32)


def kernel(
    nseq, nz, heads, rows,
    k_in, v_in, q_in, c_in, near_ref,
    o_out, gq_out, gk_out, gv_out,
    kx, vx, qb, cb, o_st, gq_st, gk_st, gv_st, g_out, g_in, s_buf, gk_acc, gv_acc, bias_ref, own,
    in_send, in_recv, in_loc, halo_send, halo_recv, g_send, g_recv, out_send, out_recv, out_loc,
):
    s = lax.axis_index("seq")
    z = lax.axis_index("head")
    has_prev = s > 0
    has_next = s < nseq - 1
    scale = 1.0 / math.sqrt(HD)
    log2_scale = scale * math.log2(math.e)

    far_first = sorted(range(1, nz), key=lambda d: abs(2 * d - nz))
    peers = [lax.rem(z + d, nz) for d in far_first]
    ins = (k_in, v_in, q_in, c_in)
    outs = (o_out, gq_out, gk_out, gv_out)
    stages = (o_st, gq_st, gk_st, gv_st)

    def in_place(a, h, source):
        if a < 2:
            start = FRAME + source * rows
            return (kx, vx)[a].at[h, pl.ds(pl.multiple_of(start, 32), rows), :]
        return (qb, cb)[a - 2].at[h, pl.ds(pl.multiple_of(source * rows, 32), rows), :]

    def columns(owner, h):
        return pl.ds(pl.multiple_of((owner * heads + h) * HD, HD), HD)

    def in_copy(a, h, peer, source):
        return pltpu.make_async_remote_copy(
            src_ref=ins[a].at[:, columns(peer, h)],
            dst_ref=in_place(a, h, source),
            send_sem=in_send.at[a, h, peer],
            recv_sem=in_recv.at[a, h, source],
            device_id=(s, peer),
            device_id_type=MESH,
        )

    def in_local(a, h):
        return pltpu.make_async_copy(
            ins[a].at[:, columns(z, h)], in_place(a, h, z), in_loc.at[a, h]
        )

    def out_copy(a, h, peer, source):
        return pltpu.make_async_remote_copy(
            src_ref=stages[a].at[h, pl.ds(pl.multiple_of(peer * rows, 32), rows), :],
            dst_ref=outs[a].at[:, columns(source, h)],
            send_sem=out_send.at[a, h, peer],
            recv_sem=out_recv.at[a, h, source],
            device_id=(s, peer),
            device_id_type=MESH,
        )

    def out_local(a, h):
        return pltpu.make_async_copy(
            stages[a].at[h, pl.ds(pl.multiple_of(z * rows, 32), rows), :],
            outs[a].at[:, columns(z, h)],
            out_loc.at[a, h],
        )

    def halo_copy(a, h, side):
        ext = (kx, vx)[a]
        return pltpu.make_async_remote_copy(
            src_ref=ext.at[h, pl.ds(FRAME, FRAME), :],
            dst_ref=ext.at[h, pl.ds(2 * FRAME * side, FRAME), :],
            send_sem=halo_send.at[a, h, side],
            recv_sem=halo_recv.at[a, h, side],
            device_id=(s + 1 - 2 * side, z),
            device_id_type=MESH,
        )

    def grad_copy(a, h, side):
        return pltpu.make_async_remote_copy(
            src_ref=g_out.at[a, h, side],
            dst_ref=g_in.at[a, h, side],
            send_sem=g_send.at[a, h, side],
            recv_sem=g_recv.at[a, h, side],
            device_id=(s - 1 + 2 * side, z),
            device_id_type=MESH,
        )

    barrier = pltpu.get_barrier_semaphore()
    for peer in peers:
        pl.semaphore_signal(barrier, inc=1, device_id=(s, peer), device_id_type=MESH)

    @pl.when(has_prev)
    def _():
        pl.semaphore_signal(barrier, inc=1, device_id=(s - 1, z), device_id_type=MESH)

    @pl.when(has_next)
    def _():
        pl.semaphore_signal(barrier, inc=1, device_id=(s + 1, z), device_id_type=MESH)

    pl.semaphore_wait(barrier, nz - 1 + has_prev.astype(jnp.int32) + has_next.astype(jnp.int32))

    def start_in(h):
        for a in range(4):
            for peer in peers:
                in_copy(a, h, peer, z).start()
            in_local(a, h).start()

    start_in(0)

    first_tile = s * TILES_F
    ext_rows = 40
    listed = near_ref[...]
    count = listed.shape[1]
    ext_row = lax.broadcasted_iota(jnp.int32, (ext_rows, count), 0)
    present = jnp.zeros((ext_rows, count), F32)
    for k in range(3 * TILES_F):
        tile = first_tile - TILES_F + k
        match = (listed == tile) & (listed >= 0)
        match = jnp.max(jnp.where(match, 1.0, 0.0).astype(F32), axis=0, keepdims=True)
        present = jnp.where(ext_row == k, match, present)
    present = present.astype(BF16)
    tile_row = lax.broadcasted_iota(jnp.int32, (count, ROW), 0)
    lane_tile = first_tile + lax.broadcasted_iota(jnp.int32, (count, ROW), 1) // TILE
    for r in range(TILE_ROWS):
        spread = jnp.where(tile_row == lane_tile + r * TILE_COLS, 1.0, 0.0).astype(BF16)
        bias = jnp.where(dot(present, spread, NN) > 0.5, 0.0, masked_score).astype(F32)
        for n in range(3 * TILE_ROWS):
            bias_ref[r, n, 0:TILE_COLS, :] = bias[n * TILE_COLS : (n + 1) * TILE_COLS, :]

    @pl.when(jnp.logical_not(has_prev))
    def _():
        kx[:, 0:FRAME, :] = jnp.zeros((heads, FRAME, HD), BF16)
        vx[:, 0:FRAME, :] = jnp.zeros((heads, FRAME, HD), BF16)

    @pl.when(jnp.logical_not(has_next))
    def _():
        kx[:, 2 * FRAME : 3 * FRAME, :] = jnp.zeros((heads, FRAME, HD), BF16)
        vx[:, 2 * FRAME : 3 * FRAME, :] = jnp.zeros((heads, FRAME, HD), BF16)

    def wait_in(h, arrays):
        for a in arrays:
            for peer in peers:
                in_copy(a, h, peer, peer).wait_recv()
            in_local(a, h).wait()

    def forward(h):
        wait_in(h, (0, 1))
        for side, there in ((0, has_next), (1, has_prev)):
            @pl.when(there)
            def _(side=side):
                for a in range(2):
                    halo_copy(a, h, side).start()

        @pl.when(h + 1 < heads)
        def _():
            start_in(h + 1)

    def attend(h, r):
        low, high = max(r - 1, 0), min(r + 1, TILE_ROWS - 1)
        near = range(low, high + 1)
        base = r * ROW
        q = qb[h, base : base + ROW, :]
        c = cb[h, base : base + ROW, :]

        def first(f, top):
            for n in near:
                start = pl.multiple_of(f * FRAME + n * ROW, ROW)
                t = dot(kx[h, pl.ds(start, ROW), :], q, NT) * log2_scale
                rows_bias = bias_ref[r, f * TILE_ROWS + n]
                parts = []
                for k in range(TILE_COLS):
                    part = t[k * TILE : (k + 1) * TILE, :] + rows_bias[k : k + 1, :]
                    s_buf[pl.ds(start + k * TILE, TILE), :] = part
                    top = jnp.maximum(top, jnp.max(part.reshape(TILE // 8, 8, ROW), axis=0))
            return top

        top = lax.fori_loop(0, 3, first, jnp.full((8, ROW), masked_score, F32))
        top = jnp.max(top, axis=0, keepdims=True)

        def second(f, carry):
            total, out_t = carry
            for n in near:
                start = pl.multiple_of(f * FRAME + n * ROW, ROW)
                e = jnp.exp2(s_buf[pl.ds(start, ROW), :] - top)
                s_buf[pl.ds(start, ROW), :] = e
                total = total + jnp.sum(e.reshape(ROW // 8, 8, ROW), axis=0)
                out_t = out_t + dot(vx[h, pl.ds(start, ROW), :], e.astype(BF16), TN)
            return total, out_t

        total, out_t = lax.fori_loop(
            0, 3, second, (jnp.zeros((8, ROW), F32), jnp.zeros((HD, ROW), F32))
        )
        inverse = 1.0 / jnp.sum(total, axis=0, keepdims=True)
        out = jnp.transpose(out_t * inverse).astype(BF16)
        o_st[h, base : base + ROW, :] = out
        products = jnp.transpose(out.astype(F32) * c.astype(F32))
        grad_dot = jnp.sum(products, axis=0, keepdims=True)
        inverse_scaled = inverse * scale

        def third(f, gq_t):
            for n in near:
                start = pl.multiple_of(f * FRAME + n * ROW, ROW)
                here = pl.ds(start, ROW)
                e = s_buf[here, :]
                gp = dot(vx[h, here, :], c, NT)
                p_low = (e * inverse).astype(BF16)
                gs = ((e * inverse_scaled) * (gp - grad_dot)).astype(BF16)
                gv = dot(p_low, c, NN)
                gk = dot(gs, q, NN)
                if r == max(n - 1, 0):
                    gv_acc[here, :] = gv
                    gk_acc[here, :] = gk
                else:
                    gv_acc[here, :] += gv
                    gk_acc[here, :] += gk
                gq_t = gq_t + dot(kx[h, here, :], gs, TN)
            return gq_t

        gq_t = lax.fori_loop(0, 3, third, jnp.zeros((HD, ROW), F32))
        gq_st[h, base : base + ROW, :] = jnp.transpose(gq_t).astype(BF16)

    def send_out(a, h):
        for peer in peers:
            out_copy(a, h, peer, z).start()
        out_local(a, h).start()

    def finish(h):
        for side, there in ((1, has_prev), (0, has_next)):
            @pl.when(there)
            def _(side=side):
                for a in range(2):
                    grad_copy(a, h, side).wait_recv()
                    own[a] += g_in[a, h, side].astype(F32)
        for a in range(2):
            stages[2 + a][h] = own[a].astype(BF16)

    forward(0)

    def one_head(h, _):
        wait_in(h, (2, 3))
        for side, there in ((0, has_prev), (1, has_next)):
            @pl.when(there)
            def _(side=side):
                for a in range(2):
                    halo_copy(a, h, side).wait_recv()

        attend(h, 0)
        attend(h, 1)

        @pl.when(h + 1 < heads)
        def _():
            forward(h + 1)

        @pl.when(h > 0)
        def _():
            finish(h - 1)
            send_out(2, h - 1)
            send_out(3, h - 1)

        attend(h, 2)
        for a in range(2):
            own[a] = (gk_acc, gv_acc)[a][FRAME : 2 * FRAME, :]
        for side, there in ((0, has_prev), (1, has_next)):
            @pl.when(there)
            def _(side=side):
                for a in range(2):
                    part = (gk_acc, gv_acc)[a][pl.ds(2 * FRAME * side, FRAME), :]
                    g_out[a, h, side] = part.astype(BF16)
                    grad_copy(a, h, side).start()

        send_out(0, h)
        send_out(1, h)
        return 0

    lax.fori_loop(0, heads, one_head, 0)
    finish(heads - 1)
    send_out(2, heads - 1)
    send_out(3, heads - 1)

    def drain(h, _):
        for a in range(4):
            for peer in peers:
                in_copy(a, h, peer, z).wait_send()
                out_copy(a, h, peer, z).wait_send()
                out_copy(a, h, peer, peer).wait_recv()
            out_local(a, h).wait()
        for a in range(2):
            for side, there, back in ((0, has_next, has_prev), (1, has_prev, has_next)):
                @pl.when(there)
                def _(a=a, side=side):
                    halo_copy(a, h, side).wait_send()

                @pl.when(back)
                def _(a=a, side=side):
                    grad_copy(a, h, side).wait_send()
        return 0

    lax.fori_loop(0, heads, drain, 0)


def place_results(*refs):
    for a in range(4):
        refs[4 + a][...] = refs[a][...]


def shards(nseq, nz, queries, keys, values, cotangent, neighbours):
    rows, width = queries.shape
    heads = width // HD // nz
    place = pl.BlockSpec(memory_space=pl.ANY)
    dma = pltpu.SemaphoreType.DMA
    results = pl.pallas_call(
        functools.partial(kernel, nseq, nz, heads, rows),
        out_shape=[jax.ShapeDtypeStruct((rows, width), BF16)] * 4,
        in_specs=[place] * 4 + [pl.BlockSpec(memory_space=pltpu.VMEM)],
        out_specs=[place] * 4,
        scratch_shapes=[
            pltpu.VMEM((heads, 3 * FRAME, HD), BF16),
            pltpu.VMEM((heads, 3 * FRAME, HD), BF16),
            pltpu.VMEM((heads, FRAME, HD), BF16),
            pltpu.VMEM((heads, FRAME, HD), BF16),
            pltpu.VMEM((heads, FRAME, HD), BF16),
            pltpu.VMEM((heads, FRAME, HD), BF16),
            pltpu.VMEM((heads, FRAME, HD), BF16),
            pltpu.VMEM((heads, FRAME, HD), BF16),
            pltpu.VMEM((2, heads, 2, FRAME, HD), BF16),
            pltpu.VMEM((2, heads, 2, FRAME, HD), BF16),
            pltpu.VMEM((3 * FRAME, ROW), F32),
            pltpu.VMEM((3 * FRAME, HD), F32),
            pltpu.VMEM((3 * FRAME, HD), F32),
            pltpu.VMEM((TILE_ROWS, 3 * TILE_ROWS, 8, ROW), F32),
            pltpu.VMEM((2, FRAME, HD), F32),
            dma((4, heads, nz)),
            dma((4, heads, nz)),
            dma((4, heads)),
            dma((2, heads, 2)),
            dma((2, heads, 2)),
            dma((2, heads, 2)),
            dma((2, heads, 2)),
            dma((4, heads, nz)),
            dma((4, heads, nz)),
            dma((4, heads)),
        ],
        compiler_params=pltpu.CompilerParams(
            collective_id=0, has_side_effects=True, vmem_limit_bytes=56 * 1024 * 1024
        ),
    )(keys, values, queries, cotangent, neighbours.T)
    block_rows = 48 if rows % 48 == 0 else rows
    block = pl.BlockSpec((block_rows, width), lambda i: (i, 0))
    return pl.pallas_call(
        place_results,
        grid=(rows // block_rows,),
        out_shape=[jax.ShapeDtypeStruct((rows, width), BF16)] * 4,
        in_specs=[block] * 4,
        out_specs=[block] * 4,
        compiler_params=pltpu.CompilerParams(vmem_limit_bytes=56 * 1024 * 1024),
    )(*results)


def solution(mesh):
    placed = P(("seq", "head"), None)
    return jax.shard_map(
        functools.partial(shards, mesh.shape["seq"], mesh.shape["head"]),
        mesh=mesh,
        in_specs=(placed, placed, placed, placed, P()),
        out_specs=(placed, placed, placed, placed),
        check_vma=False,
    )
```
